256 devices in a mesh: vrow: 16 (over z, core), vcol: 8 (over y, x_lo), pair: 2 (over x_hi).
Axes of the slice: x: 4 (x_hi: 2, x_lo: 2; x = x_hi * 2 + x_lo), y: 4, z: 8, core: 2. Of those that a mesh axis runs over, the one named last changes fastest.
Arguments:
- vertex: bfloat16 [1024, 1024, 500], P('vrow', 'vcol'), may hold values from -0.125 to 0.125
- amps: bfloat16 [192, 8, 1024], P('pair', None, 'vcol'), may hold values from -6 to 6
Outputs:
- ladder: float32 [192, 1024, 1024], P('pair', ('vrow', 'vcol'))
The draws below stay inside these ranges and needn't reach their ends.
All inputs are finite; a program needn't handle non-finite values.
Results may differ from the reference program's by a relative error of at most 0.0029.
Values may be sent and summed in bfloat16 or wider, within the bound.
No kernel may reach another device: no remote copies, remote signals or barrier semaphores. Data moves between devices by JAX's collectives and lax.ppermute only.
A program may use at most 128 MiB of HBM per device.

```python
import jax
import jax.numpy as jnp
from jax import lax

NV = 1024
NG = 500
NC = 8
NP = 192
N_VROW = 16
N_VCOL = 8


def steps_of(stream_key, extent, cuts, least, top_value):
    factor_of = 1.0
    for dim, blocks in cuts:
        draws = jax.random.uniform(jax.random.fold_in(jax.random.fold_in(stream_key, 6), dim), (blocks,), jnp.float32, least / len(cuts), top_value / len(cuts))
        factor_of = factor_of * jnp.repeat(jnp.exp(draws), extent[dim] // blocks).reshape((-1,) + (1,) * (len(extent) - 1 - dim))
    return factor_of


def normal_values(rng, shape, deviation, most, shards=(), kind=jnp.bfloat16):
    result = jax.random.normal(rng, shape, jnp.float32) * deviation
    if len(shards) > 0:
        result = steps_of(rng, shape, shards, -0.22, 0.18) * result
    return jnp.clip(result, min=-most, max=most).astype(kind)


def setup_inputs(seed: int = 0) -> dict:
    arg_keys = jax.random.split(jax.random.key(seed), 3)
    vertex = normal_values(arg_keys[0], (NV, NV, NG), (2 * NV) ** -0.5, 0.125, ((0, 16), (1, 8)))
    amps = normal_values(arg_keys[1], (NP, NC, NV), 1.0, 6.0, ((0, 2), (2, 8)))
    return {"vertex": vertex, "amps": amps}


def reference(vertex, amps):
    row_count = NV // (N_VROW * N_VCOL)
    window = vertex[:, :NC, :].astype(jnp.float32)
    amp_float = amps.astype(jnp.float32)

    def one_block(block_index):
        vertex_block = lax.dynamic_slice_in_dim(vertex, block_index * row_count, row_count, 0).astype(jnp.float32)
        inner_terms = jnp.einsum('pcd,bdg->pcbg', amp_float, vertex_block, precision=lax.Precision.HIGHEST)
        inner_terms = lax.optimization_barrier(inner_terms.astype(jnp.bfloat16)).astype(jnp.float32)
        return jnp.einsum('pcbg,acg->pba', inner_terms, window, precision=lax.Precision.HIGHEST)

    blocks = lax.map(one_block, jnp.arange(N_VROW * N_VCOL, dtype=jnp.int32))
    return jnp.transpose(blocks, (1, 0, 2, 3)).reshape(NP, NV, NV)
```

```python
import jax
import jax.numpy as jnp
from jax import lax
from jax.experimental import pallas as pl
from jax.experimental.pallas import tpu as pltpu
from jax.sharding import PartitionSpec as P

NC = 8
AXES = ("vrow", "vcol", "pair")
MIB = 1 << 20


def flat(x, y, z, c):
    x, y, z, c = x % 4, y % 4, z % 8, c % 2
    return ((z * 2 + c) * 8 + (y * 2 + x % 2)) * 2 + x // 2


def send(value, move, only=lambda x, y: True):
    pairs = []
    for x in range(4):
        for y in range(4):
            if not only(x, y):
                continue
            for z in range(8):
                for c in range(2):
                    pairs.append((flat(x, y, z, c), flat(*move(x, y, z, c))))
    return lax.ppermute(value, AXES, pairs)


def step(dx=0, dy=0, dz=0, dc=0):
    return lambda x, y, z, c: (x + dx, y + dy, z + dz, c + dc)


def inner_kernel(mine_ref, other_ref, v_ref, out_ref, t_ref):
    core = lax.rem(lax.axis_index("vrow"), 2)
    pair = lax.axis_index("pair")

    @pl.when(pl.program_id(0) == 0)
    def _():
        for src, own in ((mine_ref, core), (other_ref, 1 - core)):
            for j in range(8):
                for k in range(2):
                    kk = lax.rem(pair + k, 2)
                    for c in range(4):
                        t_ref[own * 4 + c, kk, :, j * 128 : (j + 1) * 128] = src[j * 2 + k, c]

    v = jnp.concatenate([v_ref[j, 0] for j in range(8)], axis=-1)
    t = t_ref[...].reshape(NC * 192, 1024)
    prod = lax.dot_general(t, v, (((1,), (1,)), ((), ())), preferred_element_type=jnp.float32)
    out_ref[...] = prod.astype(jnp.bfloat16).reshape(NC, 1, 2, 96, 500)


def inner_terms(mine, other, v):
    nb = v.shape[1]
    return pl.pallas_call(
        inner_kernel,
        grid=(nb,),
        in_specs=[
            pl.BlockSpec((16, 4, 96, 128), lambda b: (0, 0, 0, 0)),
            pl.BlockSpec((16, 4, 96, 128), lambda b: (0, 0, 0, 0)),
            pl.BlockSpec((8, 1, 500, 128), lambda b: (0, b, 0, 0)),
        ],
        out_specs=pl.BlockSpec((NC, 1, 2, 96, 500), lambda b: (0, b, 0, 0, 0)),
        out_shape=jax.ShapeDtypeStruct((NC, nb, 2, 96, 500), jnp.bfloat16),
        scratch_shapes=[pltpu.VMEM((NC, 2, 96, 1024), jnp.bfloat16)],
        compiler_params=pltpu.CompilerParams(vmem_limit_bytes=48 * MIB),
        cost_estimate=pl.CostEstimate(flops=2 * nb * 1536 * 1024 * 512, bytes_accessed=8 * MIB, transcendentals=0),
    )(mine, other, v)


def ladder_kernel(s_ref, a_ref, b_ref, own_ref, far_ref, acc_ref):
    core = lax.rem(lax.axis_index("vrow"), 2)
    rows = s_ref.shape[1] * 192
    total = None
    for i, src in enumerate((a_ref, b_ref)):
        own = core if i == 0 else 1 - core
        for c in range(4):
            lhs = s_ref[own * 4 + c].reshape(rows, 500)
            p = jnp.dot(lhs, src[c], preferred_element_type=jnp.float32)
            total = p if total is None else total + p
    total = total.reshape(s_ref.shape[1], 2, 96, -1)
    own_ref[...] = total[:, 0]
    far_ref[...] = total[:, 1].astype(jnp.bfloat16)


def ladder_part(s, w_own, w_far):
    nb, na = s.shape[1], w_own.shape[2]
    return pl.pallas_call(
        ladder_kernel,
        out_shape=(
            jax.ShapeDtypeStruct((nb, 96, na), jnp.float32),
            jax.ShapeDtypeStruct((nb, 96, na), jnp.bfloat16),
        ),
        scratch_shapes=[pltpu.VMEM((8, 128), jnp.float32)],
        compiler_params=pltpu.CompilerParams(vmem_limit_bytes=48 * MIB),
        cost_estimate=pl.CostEstimate(flops=2 * nb * 192 * 4096 * na, bytes_accessed=8 * MIB, transcendentals=0),
    )(s, w_own, w_far)


def per_device(vertex, amps):
    vrow, vcol, pair = (lax.axis_index(a) for a in AXES)
    z, core = vrow // 2, lax.rem(vrow, 2)
    y, x_lo = vcol // 2, lax.rem(vcol, 2)

    t = jnp.transpose(amps, (1, 0, 2))
    t = lax.dynamic_slice_in_dim(t, core * 4, 4, 0)
    t = jnp.broadcast_to(t[None], (16, 4, 96, 128))
    t_own = lax.all_to_all(t, ("vcol", "pair"), 0, 0, tiled=True)
    t_far = send(t_own, step(dc=1))

    w = jnp.transpose(vertex[:, :NC, :], (1, 2, 0))
    w_keep = lax.dynamic_slice_in_dim(w, core * 4, 4, 0)
    w_give = lax.dynamic_slice_in_dim(w, (1 - core) * 4, 4, 0)
    w_got = send(w_give, step(dc=1))
    w = jnp.where(core == 0, jnp.concatenate([w_keep, w_got], 2), jnp.concatenate([w_got, w_keep], 2))

    v = lax.dynamic_slice_in_dim(vertex.reshape(8, 2, 4, 128, 500), pair, 1, 1)[:, 0]
    v = jnp.transpose(v, (0, 1, 3, 2))
    v = lax.all_to_all(v, "vcol", 0, 0, tiled=True)

    even = lambda x: x % 2 == 0
    up = send(w, step(dy=1), lambda x, y: even(x) and y == 0)
    down = send(w, step(dy=-1), lambda x, y: even(x) and y == 0)
    w = jnp.where(y == 0, w, jnp.where(y == 1, up, down))
    up = send(w[:2], step(dy=1), lambda x, y: even(x) and y == 1)
    down = send(w[2:], step(dy=-1), lambda x, y: even(x) and y == 3)
    w = jnp.where(y == 2, jnp.concatenate([up, down], 0), w)
    up = send(w[:2], step(dx=1), lambda x, y: even(x))
    down = send(w[2:], step(dx=-1), lambda x, y: even(x))
    w = jnp.where(x_lo == 1, jnp.concatenate([up, down], 0), w)

    ups, downs = [w], [w]
    for _ in range(3):
        ups.append(send(ups[-1], step(dz=1)))
        downs.append(send(downs[-1], step(dz=-1)))
    opposite = jnp.concatenate([send(ups[-1][:2], step(dz=1)), send(downs[-1][2:], step(dz=-1))], 0)

    s = inner_terms(t_own, t_far, v)

    parts = [(w, opposite, 0, 4)] + [(ups[i], downs[i], -i, i) for i in (1, 2, 3)]
    order = [None] * 8
    for first, second, d1, d2 in (parts[1], parts[2], parts[3], parts[0]):
        blocks = jnp.concatenate([first, second], 2)
        far = send(blocks, step(dc=1))
        mine, theirs = ladder_part(s, blocks, far)
        got = send(theirs, step(dx=2)).astype(jnp.float32)
        full = jnp.where(pair == 0, jnp.concatenate([mine, got], 0), jnp.concatenate([got, mine], 0))
        full = jnp.transpose(full, (1, 0, 2))
        order[d1 % 8] = full[..., :128]
        order[d2 % 8] = full[..., 128:]
    out = jnp.concatenate(order + order, 2)
    return lax.dynamic_slice_in_dim(out, lax.rem(8 - z, 8) * 128, 1024, 2)


def solution(mesh):
    return jax.shard_map(
        per_device,
        mesh=mesh,
        in_specs=(P("vrow", "vcol", None), P("pair", None, "vcol")),
        out_specs=P("pair", ("vrow", "vcol"), None),
        check_vma=False,
    )
```

```python
import jax
import jax.numpy as jnp
from jax import lax
from jax.experimental import pallas as pl
from jax.experimental.pallas import tpu as pltpu
from jax.sharding import Mesh, PartitionSpec as P

NC, NG = 8, 500
AXES = ("z", "core", "y", "x_lo", "pair")
SIZES = (8, 2, 4, 2, 2)
MIB = 1 << 20
F32, BF16 = jnp.float32, jnp.bfloat16
CHUNKS = ((0, 2), (2, 2))


def flat(x, y, z, c):
    x, y, z, c = x % 4, y % 4, z % 8, c % 2
    return ((z * 2 + c) * 8 + (y * 2 + x % 2)) * 2 + x // 2


def send(value, dx=0, dy=0, dz=0, dc=0):
    pairs = [
        (flat(x, y, z, c), flat(x + dx, y + dy, z + dz, c + dc))
        for x in range(4)
        for y in range(4)
        for z in range(8)
        for c in range(2)
    ]
    return lax.ppermute(value, AXES, pairs)


def exchange(value, axes):
    return lax.all_to_all(value, axes, 0, 0, tiled=True)


def params(mib=48):
    return pltpu.CompilerParams(vmem_limit_bytes=mib * MIB)


def cost(flops, nbytes):
    return pl.CostEstimate(flops=flops, bytes_accessed=nbytes, transcendentals=0)


def extract_kernel(lo_ref, hi_ref, sel_ref, *rest):
    v_refs, w_ref, f_ref = rest[:-2], rest[-2], rest[-1]
    first = 4 * lax.axis_index("pair")
    g = lax.broadcasted_iota(jnp.int32, (16, 64, 128), 0) + (256 + 16 * pl.program_id(0))
    halves = (lo_ref[...], jnp.where(g < NG, hi_ref[...], 0))
    for h, x in enumerate(halves):
        f_ref[h] = x.astype(F32).reshape(16 * 64, 128)
    for h in range(2):
        for j in range(8):
            for (start, count), v_ref in zip(CHUNKS, v_refs):
                for b in range(count):
                    row = f_ref[h, pl.ds(8 * j + first + start + b, 16, stride=64), :]
                    v_ref[j, b, h] = row.astype(BF16)
    lhs = jnp.concatenate(
        [jnp.concatenate([halves[0][i], halves[1][i]], axis=0) for i in range(16)], axis=1
    )
    picked = jnp.dot(lhs, sel_ref[...], preferred_element_type=F32)
    w_ref[...] = jnp.transpose(picked).astype(BF16).reshape(NC, 16, 128)


def extract(vertex):
    by_g = jnp.transpose(vertex, (2, 0, 1))
    i, d = jnp.arange(2048) // 128, jnp.arange(2048) % 128
    c2, i2 = jnp.arange(128) // 16, jnp.arange(128) % 16
    sel = ((i[:, None] == i2[None]) & (d[:, None] == c2[None])).astype(BF16)
    outs = pl.pallas_call(
        extract_kernel,
        grid=(16,),
        in_specs=[
            pl.BlockSpec((16, 64, 128), lambda u: (u, 0, 0)),
            pl.BlockSpec((16, 64, 128), lambda u: (16 + u, 0, 0)),
            pl.BlockSpec((2048, 128), lambda u: (0, 0)),
        ],
        out_specs=[pl.BlockSpec((8, n, 2, 16, 128), lambda u: (0, 0, 0, u, 0)) for _, n in CHUNKS]
        + [pl.BlockSpec((NC, 16, 128), lambda u: (0, u, 0))],
        out_shape=[jax.ShapeDtypeStruct((8, n, 2, 256, 128), BF16) for _, n in CHUNKS]
        + [jax.ShapeDtypeStruct((NC, 256, 128), BF16)],
        scratch_shapes=[pltpu.VMEM((2, 16 * 64, 128), F32)],
        compiler_params=params(),
        cost_estimate=cost(2 * 2048 * 2048 * 128, 14 * MIB),
    )(by_g, by_g, sel)
    return outs[:-1], outs[-1]


def amps_kernel(mine_ref, other_ref, t_ref):
    core, pair = lax.axis_index("core"), lax.axis_index("pair")
    for src, own in ((mine_ref, core), (other_ref, 1 - core)):
        for x in range(4):
            for y in range(4):
                j, k = y * 2 + x // 2, x % 2
                for c in range(4):
                    t_ref[own * 4 + c, lax.rem(pair + k, 2), :, j * 128 : (j + 1) * 128] = src[x, y, c]


def gather_amps(mine, other):
    return pl.pallas_call(
        amps_kernel,
        out_shape=jax.ShapeDtypeStruct((NC, 2, 96, 1024), BF16),
        compiler_params=params(),
        cost_estimate=cost(0, 7 * MIB),
    )(mine, other)


def inner_kernel(t_ref, v_ref, out_ref):
    v = jnp.concatenate([v_ref[j, 0].reshape(512, 128) for j in range(8)], axis=-1)
    t = t_ref[...].reshape(NC * 192, 1024)
    prod = lax.dot_general(t, v, (((1,), (1,)), ((), ())), preferred_element_type=F32)
    out_ref[...] = prod.astype(BF16).reshape(NC, 1, 192, 512)


def inner_terms(t, v):
    nb = v.shape[1]
    return pl.pallas_call(
        inner_kernel,
        grid=(nb,),
        in_specs=[
            pl.BlockSpec((NC, 2, 96, 1024), lambda b: (0, 0, 0, 0)),
            pl.BlockSpec((8, 1, 2, 256, 128), lambda b: (0, b, 0, 0, 0)),
        ],
        out_specs=pl.BlockSpec((NC, 1, 192, 512), lambda b: (0, b, 0, 0)),
        out_shape=jax.ShapeDtypeStruct((NC, nb, 192, 512), BF16),
        compiler_params=params(),
        cost_estimate=cost(2 * nb * 1536 * 1024 * 512, 8 * MIB),
    )(t, v)


def ladder_kernel(*refs):
    s_refs, (mine0, mine1, far0, far1, own_ref, give_ref) = refs[:-6], refs[-6:]
    core = lax.axis_index("core")
    low = lax.broadcasted_iota(jnp.int32, (256, 128), 1) < 64
    totals = [None] * len(s_refs)
    for c in range(NC):
        weights = []
        for mine_ref, far_ref in ((mine0, far0), (mine1, far1)):
            mine, far = mine_ref[c].astype(F32), far_ref[c].astype(F32)
            one = jnp.where(core == 0, mine, far)
            two = jnp.where(core == 0, far, mine)
            lo = jnp.where(low, one, pltpu.roll(two, 64, 1))
            hi = jnp.where(low, pltpu.roll(one, 64, 1), two)
            weights.append(jnp.concatenate([lo, hi], axis=0).astype(BF16))
        weight = jnp.concatenate(weights, axis=1)
        for n, s_ref in enumerate(s_refs):
            lhs = s_ref[c].reshape(-1, 512)
            p = jnp.dot(lhs, weight, preferred_element_type=F32)
            totals[n] = p if totals[n] is None else totals[n] + p
    row = 0
    for total in totals:
        total = total.reshape(-1, 2, 96, 256)
        n = total.shape[0]
        own_ref[row : row + n] = total[:, 0]
        give_ref[row : row + n] = total[:, 1].astype(BF16)
        row += n


def ladder_part(inner, mine, far):
    return pl.pallas_call(
        ladder_kernel,
        out_shape=(
            jax.ShapeDtypeStruct((4, 96, 256), F32),
            jax.ShapeDtypeStruct((4, 96, 256), BF16),
        ),
        compiler_params=params(),
        cost_estimate=cost(2 * 768 * 4096 * 256, 10 * MIB),
    )(*inner, *mine, *far)


def assemble_kernel(*refs):
    own_refs, got_refs, out_ref = refs[:4], refs[4:8], refs[8]
    z, pair = lax.axis_index("z"), lax.axis_index("pair")

    def place(mine, theirs):
        for i, (own_ref, got_ref) in enumerate(zip(own_refs, got_refs)):
            for h, shift in enumerate(SHIFTS[i]):
                start = pl.multiple_of(lax.rem(z + 8 + shift, 8) * 128, 128)
                for b in range(4):
                    lanes = slice(h * 128, (h + 1) * 128)
                    out_ref[:, mine + b, pl.ds(start, 128)] = own_ref[b, :, lanes]
                    out_ref[:, theirs + b, pl.ds(start, 128)] = got_ref[b, :, lanes].astype(F32)

    @pl.when(pair == 0)
    def _():
        place(0, 4)

    @pl.when(pair == 1)
    def _():
        place(4, 0)


SHIFTS = ((-1, 1), (-2, 2), (-3, 3), (0, 4))


def assemble(own, got):
    return pl.pallas_call(
        assemble_kernel,
        grid=(6,),
        in_specs=[pl.BlockSpec((4, 16, 256), lambda p: (0, p, 0))] * 8,
        out_specs=pl.BlockSpec((16, 8, 1024), lambda p: (p, 0, 0)),
        out_shape=jax.ShapeDtypeStruct((96, 8, 1024), F32),
        compiler_params=params(),
        cost_estimate=cost(0, 6 * MIB),
    )(*own, *got)


def per_device(vertex, amps):
    core, pair = lax.axis_index("core"), lax.axis_index("pair")
    chunks, w = extract(vertex)

    piece = exchange(w.reshape(16, 128, 128), ("y", "x_lo", "pair"))
    piece = lax.dynamic_slice_in_dim(piece, pair, 1, 0)
    w = exchange(jnp.broadcast_to(piece, (16, 128, 128)), ("y", "x_lo", "pair"))
    w = w.reshape(NC, 256, 128)

    t = jnp.transpose(amps, (1, 0, 2))
    t = lax.dynamic_slice_in_dim(t, core * 4, 4, 0)
    t = exchange(jnp.broadcast_to(t[None], (4, 4, 96, 128)), "y")
    t = exchange(jnp.broadcast_to(t[None], (4, 4, 4, 96, 128)).reshape(4, 4, 4, 96, 128), ("x_lo", "pair"))
    t = gather_amps(t, send(t, dc=1))

    inner = [inner_terms(t, exchange(v, ("y", "x_lo"))) for v in chunks]

    ups, downs = [w], [w]
    for _ in range(3):
        ups.append(send(ups[-1], dz=1))
        downs.append(send(downs[-1], dz=-1))
    opposite = jnp.concatenate([send(ups[-1][:4], dz=1), send(downs[-1][4:], dz=-1)], 0)

    own, got = [], []
    for blocks in [(ups[i], downs[i]) for i in (1, 2, 3)] + [(w, opposite)]:
        far = [send(block, dc=1) for block in blocks]
        mine, give = ladder_part(inner, blocks, far)
        own.append(mine)
        got.append(send(give, dx=2))
    return assemble(own, got)


def solution(mesh):
    fine = Mesh(mesh.devices.reshape(SIZES), AXES)
    return jax.shard_map(
        per_device,
        mesh=fine,
        in_specs=(P(("z", "core"), ("y", "x_lo"), None), P("pair", None, ("y", "x_lo"))),
        out_specs=P("pair", ("z", "core", "y", "x_lo"), None),
        check_vma=False,
    )
```

```python
import jax
import jax.numpy as jnp
import numpy as np
from jax import lax
from jax.experimental import pallas as pl
from jax.experimental.pallas import tpu as pltpu
from jax.sharding import Mesh, PartitionSpec as P

NC, NG = 8, 500
AXES = ("z", "core", "y", "x_lo", "pair")
SIZES = (8, 2, 4, 2, 2)
MIB = 1 << 20
F32, BF16 = jnp.float32, jnp.bfloat16
CHUNKS = ((0, 3), (3, 1))
SHIFTS = ((-1, 1), (-2, 2), (-3, 3), (0, 4))


def flat(x, y, z, c):
    x, y, z, c = x % 4, y % 4, z % 8, c % 2
    return ((z * 2 + c) * 8 + (y * 2 + x % 2)) * 2 + x // 2


def send(value, dx=0, dy=0, dz=0, dc=0, only=lambda x, y: True):
    pairs = [
        (flat(x, y, z, c), flat(x + dx, y + dy, z + dz, c + dc))
        for x in range(4)
        for y in range(4)
        for z in range(8)
        for c in range(2)
        if only(x, y)
    ]
    return lax.ppermute(value, AXES, pairs)


def after(value, *earlier):
    return lax.optimization_barrier((value, *earlier))[0]


def params(mib=56):
    return pltpu.CompilerParams(vmem_limit_bytes=mib * MIB)


def cost(flops, nbytes):
    return pl.CostEstimate(flops=flops, bytes_accessed=nbytes, transcendentals=0)


I, D = np.arange(2048) // 128, np.arange(2048) % 128
PICK = ((I[:, None] == np.arange(128) % 16) & (D[:, None] == np.arange(128) // 16)).astype(BF16)
R, K = np.arange(128), np.arange(256)
ROWS = np.stack(
    [
        (K[None] // 16 == R[:, None] % 16) & (K[None] % 16 == (8 * (R // 64) + 4 * k + (R // 16) % 4)[:, None])
        for k in range(2)
    ]
).astype(BF16)


def window_kernel(lo_ref, hi_ref, pick_ref, w_ref):
    for s in range(8):
        cols = []
        for i in range(16):
            hi = hi_ref[16 * s + i]
            if s == 7:
                hi = jnp.where(256 + 128 * pl.program_id(0) + 16 * s + i < NG, hi, 0)
            cols.append(jnp.concatenate([lo_ref[16 * s + i], hi], axis=0))
        picked = jnp.dot(jnp.concatenate(cols, axis=1), pick_ref[...], preferred_element_type=F32)
        w_ref[:, 16 * s : 16 * s + 16] = jnp.transpose(picked).astype(BF16).reshape(NC, 16, 128)


def window(by_g):
    return pl.pallas_call(
        window_kernel,
        grid=(2,),
        in_specs=[
            pl.BlockSpec((128, 64, 128), lambda u: (u, 0, 0)),
            pl.BlockSpec((128, 64, 128), lambda u: (2 + u, 0, 0)),
            pl.BlockSpec((2048, 128), lambda u: (0, 0)),
        ],
        out_specs=pl.BlockSpec((NC, 128, 128), lambda u: (0, u, 0)),
        out_shape=jax.ShapeDtypeStruct((NC, 256, 128), BF16),
        compiler_params=params(),
        cost_estimate=cost(2 * 2048 * 2048 * 128, 9 * MIB),
    )(by_g, by_g, jnp.asarray(PICK))


def rows_kernel(x_ref, rows_ref, *v_refs):
    pair = lax.axis_index("pair")
    for s in range(16):
        x = x_ref[16 * s : 16 * s + 16]
        if s >= 14:
            g = lax.broadcasted_iota(jnp.int32, (16, 64, 128), 0) + (256 * pl.program_id(0) + 16 * s)
            x = jnp.where(g < NG, x, 0)
        for jj in range(4):
            picked = jnp.dot(
                rows_ref[pair], x[:, 16 * jj : 16 * jj + 16].reshape(256, 128), preferred_element_type=F32
            )
            picked = picked.astype(BF16).reshape(2, 4, 16, 128)
            for (first, count), v_ref in zip(CHUNKS, v_refs):
                v_ref[2 * jj : 2 * jj + 2, :, 16 * s : 16 * s + 16] = picked[:, first : first + count]


def vertex_rows(by_g):
    return pl.pallas_call(
        rows_kernel,
        grid=(2,),
        in_specs=[
            pl.BlockSpec((256, 64, 128), lambda u: (u, 0, 0)),
            pl.BlockSpec((2, 128, 256), lambda u: (0, 0, 0)),
        ],
        out_specs=[pl.BlockSpec((8, n, 256, 128), lambda u: (0, 0, u, 0)) for _, n in CHUNKS],
        out_shape=[jax.ShapeDtypeStruct((8, n, 512, 128), BF16) for _, n in CHUNKS],
        compiler_params=params(),
        cost_estimate=cost(2 * 2048 * 2048 * 128, 13 * MIB),
    )(by_g, jnp.asarray(ROWS))


def amps_kernel(*refs):
    t_ref = refs[8]
    x = 2 * lax.axis_index("pair") + lax.axis_index("x_lo")
    y, core = lax.axis_index("y"), lax.axis_index("core")
    for half, own in ((refs[:4], core), (refs[4:8], 1 - core)):
        for dx in range(4):
            sx = lax.rem(x + dx, 4)
            k = lax.rem(sx // 2 + lax.axis_index("pair"), 2)
            for dy in range(4):
                j = lax.rem(y + dy, 4) * 2 + lax.rem(sx, 2)
                lanes = pl.ds(pl.multiple_of(j * 128, 128), 128)
                for c in range(4):
                    t_ref[own * 4 + c, k, :, lanes] = half[dx][dy, c]


def gather_amps(mine, far):
    return pl.pallas_call(
        amps_kernel,
        out_shape=jax.ShapeDtypeStruct((NC, 2, 96, 1024), BF16),
        compiler_params=params(),
        cost_estimate=cost(0, 7 * MIB),
    )(*mine, *far)


def inner_kernel(t_ref, v_ref, out_ref):
    v = jnp.concatenate([v_ref[j, 0] for j in range(8)], axis=-1)
    t = t_ref[...].reshape(NC * 192, 1024)
    prod = lax.dot_general(t, v, (((1,), (1,)), ((), ())), preferred_element_type=F32)
    out_ref[...] = prod.astype(BF16).reshape(NC, 1, 192, 512)


def inner_terms(t, v):
    nb = v.shape[1]
    return pl.pallas_call(
        inner_kernel,
        grid=(nb,),
        in_specs=[
            pl.BlockSpec((NC, 2, 96, 1024), lambda b: (0, 0, 0, 0)),
            pl.BlockSpec((8, 1, 512, 128), lambda b: (0, b, 0, 0)),
        ],
        out_specs=pl.BlockSpec((NC, 1, 192, 512), lambda b: (0, b, 0, 0)),
        out_shape=jax.ShapeDtypeStruct((NC, nb, 192, 512), BF16),
        compiler_params=params(),
        cost_estimate=cost(2 * nb * 1536 * 1024 * 512, 8 * MIB),
    )(t, v)


def ladder_kernel(n_blocks, s_ref, *refs):
    mine_refs, far_refs, (own_ref, give_ref) = refs[:n_blocks], refs[n_blocks : 2 * n_blocks], refs[2 * n_blocks :]
    core = lax.axis_index("core")
    x = 2 * lax.axis_index("pair") + lax.axis_index("x_lo")
    low = lax.broadcasted_iota(jnp.int32, (256, 128), 1) < 64
    for first in range(0, n_blocks, 2):
        total = None
        for c in range(NC):
            weights = []
            for mine_ref, far_ref in zip(mine_refs[first : first + 2], far_refs[first : first + 2]):
                mine, far = mine_ref[c].astype(F32), far_ref[c].astype(F32)
                one = jnp.where(core == 0, mine, far)
                two = jnp.where(core == 0, far, mine)
                lo = jnp.where(low, one, pltpu.roll(two, 64, 1))
                hi = jnp.where(low, pltpu.roll(one, 64, 1), two)
                weights.append(jnp.concatenate([lo, hi], axis=0).astype(BF16))
            lhs = s_ref[2 * lax.rem(x + c // 2, 4) + c % 2].reshape(-1, 512)
            p = jnp.dot(lhs, jnp.concatenate(weights, axis=1), preferred_element_type=F32)
            total = p if total is None else total + p
        total = total.reshape(-1, 2, 96, 256)
        own_ref[:, :, first * 128 : first * 128 + 256] = total[:, 0]
        give_ref[:, :, first * 128 : first * 128 + 256] = total[:, 1].astype(BF16)


def ladder_part(inner, mine, far):
    nb, na = inner.shape[1], 128 * len(mine)

    def kernel(*refs):
        ladder_kernel(len(mine), *refs)

    return pl.pallas_call(
        kernel,
        out_shape=(jax.ShapeDtypeStruct((nb, 96, na), F32), jax.ShapeDtypeStruct((nb, 96, na), BF16)),
        compiler_params=params(),
        cost_estimate=cost(2 * nb * 192 * 4096 * na, 8 * MIB),
    )(inner, *mine, *far)


def assemble_kernel(*refs):
    *pieces, out_ref = refs
    owns, gots = pieces[:5], pieces[5:]
    z, pair = lax.axis_index("z"), lax.axis_index("pair")

    def place(mine, theirs):
        for i, shift in enumerate(sum(SHIFTS, ())):
            lanes = pl.ds(pl.multiple_of(lax.rem(z + 8 + shift, 8) * 128, 128), 128)
            for b in range(4):
                if b < CHUNKS[0][1]:
                    n, row, cols = i // 2, b, slice(i % 2 * 128, i % 2 * 128 + 128)
                else:
                    n, row, cols = 4, 0, slice(i * 128, i * 128 + 128)
                out_ref[:, mine + b, lanes] = owns[n][row, :, cols]
                out_ref[:, theirs + b, lanes] = gots[n][row, :, cols].astype(F32)

    @pl.when(pair == 0)
    def _():
        place(0, 4)

    @pl.when(pair == 1)
    def _():
        place(4, 0)


def assemble(own, got):
    pieces = own + got
    return pl.pallas_call(
        assemble_kernel,
        grid=(2,),
        in_specs=[pl.BlockSpec((p.shape[0], 48, p.shape[2]), lambda i: (0, i, 0)) for p in pieces],
        out_specs=pl.BlockSpec((48, 8, 1024), lambda p: (p, 0, 0)),
        out_shape=jax.ShapeDtypeStruct((96, 8, 1024), F32),
        compiler_params=params(),
        cost_estimate=cost(0, 6 * MIB),
    )(*pieces)


def spread(w):
    y, x_lo, pair = (lax.axis_index(a) for a in ("y", "x_lo", "pair"))
    quarters = w.reshape(4, 2, 256, 128)
    keep = lax.dynamic_index_in_dim(quarters, 2 * pair, 0, False)
    give = lax.dynamic_index_in_dim(quarters, 2 * pair + 1, 0, False)
    got = send(give, dx=1, only=lambda x, y: x % 2 == 0 and y == 0)
    piece = jnp.where(x_lo == 0, keep, got)
    up, down, two = (send(piece, dy=d, only=lambda x, y: y == 0) for d in (1, -1, 2))
    piece = jnp.where(y == 0, piece, jnp.where(y == 1, up, jnp.where(y == 3, down, two)))
    rest = [send(piece, dx=-d) for d in (1, 2, 3)]
    return jnp.concatenate([piece, *rest], axis=0), got


def per_device(vertex, amps):
    core = lax.axis_index("core")
    by_g = jnp.transpose(vertex, (2, 0, 1))
    w_source = window(by_g)
    w, first_step = spread(w_source)
    v0, v1 = vertex_rows(after(by_g, w_source))
    v0 = lax.all_to_all(v0, ("y", "x_lo"), 0, 0, tiled=True)
    v1 = lax.all_to_all(after(v1, v0), ("y", "x_lo"), 0, 0, tiled=True)

    t = jnp.transpose(amps, (1, 0, 2))
    t = lax.dynamic_slice_in_dim(t, core * 4, 4, 0)
    t = after(t, first_step)
    t = jnp.stack([t] + [send(t, dy=-d) for d in (1, 2, 3)])
    t = after(t, w)
    mine = [t] + [send(t, dx=-d) for d in (1, 2, 3)]
    t = gather_amps(mine, [send(m, dc=1) for m in mine])

    ups, downs = [w], [w]
    for _ in range(3):
        ups.append(send(ups[-1], dz=1))
        downs.append(send(downs[-1], dz=-1))
    opposite = jnp.concatenate([send(ups[-1][:4], dz=1), send(downs[-1][4:], dz=-1)], 0)
    windows = []
    for blocks in [(ups[i], downs[i]) for i in (1, 2, 3)] + [(w, opposite)]:
        windows.append((blocks, tuple(send(block, dc=1) for block in blocks)))

    inner = inner_terms(t, v0)
    parts = [ladder_part(inner, *blocks) for blocks in windows]
    inner = inner_terms(t, v1)
    parts.append(ladder_part(inner, sum((b[0] for b in windows), ()), sum((b[1] for b in windows), ())))
    return assemble([own for own, _ in parts], [send(give, dx=2) for _, give in parts])


def solution(mesh):
    fine = Mesh(mesh.devices.reshape(SIZES), AXES)
    return jax.shard_map(
        per_device,
        mesh=fine,
        in_specs=(P(("z", "core"), ("y", "x_lo"), None), P("pair", None, ("y", "x_lo"))),
        out_specs=P("pair", ("z", "core", "y", "x_lo"), None),
        check_vma=False,
    )
```

```python
import jax
import jax.numpy as jnp
import numpy as np
from jax import lax
from jax.experimental import pallas as pl
from jax.experimental.pallas import tpu as pltpu
from jax.sharding import Mesh, PartitionSpec as P

NC, NG = 8, 500
AXES = ("z", "core", "y", "x_lo", "pair")
SIZES = (8, 2, 4, 2, 2)
MIB = 1 << 20
F32, BF16 = jnp.float32, jnp.bfloat16
SHIFTS = ((-1, 1), (-2, 2), (-3, 3), (0, 4))


def flat(x, y, z, c):
    x, y, z, c = x % 4, y % 4, z % 8, c % 2
    return ((z * 2 + c) * 8 + (y * 2 + x % 2)) * 2 + x // 2


def send(value, dx=0, dy=0, dz=0, dc=0, only=lambda x, y: True):
    pairs = [
        (flat(x, y, z, c), flat(x + dx, y + dy, z + dz, c + dc))
        for x in range(4)
        for y in range(4)
        for z in range(8)
        for c in range(2)
        if only(x, y)
    ]
    return lax.ppermute(value, AXES, pairs)


def after(value, *earlier):
    return lax.optimization_barrier((value, *earlier))[0]


def params(mib=24):
    return pltpu.CompilerParams(vmem_limit_bytes=mib * MIB)


def cost(flops, nbytes):
    return pl.CostEstimate(flops=flops, bytes_accessed=nbytes, transcendentals=0)


I, D = np.arange(2048) // 128, np.arange(2048) % 128
PICK = ((I[:, None] == np.arange(128) % 16) & (D[:, None] == np.arange(128) // 16)).astype(BF16)
R, K = np.arange(128), np.arange(256)
ROWS = np.stack(
    [
        (K[None] // 16 == R[:, None] % 16) & (K[None] % 16 == (8 * (R // 64) + 4 * k + (R // 16) % 4)[:, None])
        for k in range(2)
    ]
).astype(BF16)


def window_kernel(lo_ref, hi_ref, pick_ref, w_ref):
    for s in range(8):
        cols = []
        for i in range(16):
            hi = hi_ref[16 * s + i]
            if s == 7:
                hi = jnp.where(256 + 128 * pl.program_id(0) + 16 * s + i < NG, hi, 0)
            cols.append(jnp.concatenate([lo_ref[16 * s + i], hi], axis=0))
        picked = jnp.dot(jnp.concatenate(cols, axis=1), pick_ref[...], preferred_element_type=F32)
        w_ref[:, 16 * s : 16 * s + 16] = jnp.transpose(picked).astype(BF16).reshape(NC, 16, 128)


def window(by_g):
    return pl.pallas_call(
        window_kernel,
        grid=(2,),
        in_specs=[
            pl.BlockSpec((128, 64, 128), lambda u: (u, 0, 0)),
            pl.BlockSpec((128, 64, 128), lambda u: (2 + u, 0, 0)),
            pl.BlockSpec((2048, 128), lambda u: (0, 0)),
        ],
        out_specs=pl.BlockSpec((NC, 128, 128), lambda u: (0, u, 0)),
        out_shape=jax.ShapeDtypeStruct((NC, 256, 128), BF16),
        compiler_params=params(),
        cost_estimate=cost(2 * 2048 * 2048 * 128, 9 * MIB),
    )(by_g, by_g, jnp.asarray(PICK))


def rows_kernel(x_ref, rows_ref, v_ref):
    pair = lax.axis_index("pair")
    for s in range(16):
        x = x_ref[16 * s : 16 * s + 16]
        if s >= 14:
            g = lax.broadcasted_iota(jnp.int32, (16, 64, 128), 0) + (256 * pl.program_id(0) + 16 * s)
            x = jnp.where(g < NG, x, 0)
        for jj in range(4):
            picked = jnp.dot(
                rows_ref[pair], x[:, 16 * jj : 16 * jj + 16].reshape(256, 128), preferred_element_type=F32
            )
            v_ref[2 * jj : 2 * jj + 2, :, 16 * s : 16 * s + 16] = picked.astype(BF16).reshape(2, 4, 16, 128)


def vertex_rows(by_g):
    return pl.pallas_call(
        rows_kernel,
        grid=(2,),
        in_specs=[
            pl.BlockSpec((256, 64, 128), lambda u: (u, 0, 0)),
            pl.BlockSpec((2, 128, 256), lambda u: (0, 0, 0)),
        ],
        out_specs=pl.BlockSpec((8, 4, 256, 128), lambda u: (0, 0, u, 0)),
        out_shape=jax.ShapeDtypeStruct((8, 4, 512, 128), BF16),
        compiler_params=params(),
        cost_estimate=cost(2 * 2048 * 2048 * 128, 13 * MIB),
    )(by_g, jnp.asarray(ROWS))


def amps_kernel(own_ref, pair_ref, own_far_ref, pair_far_ref, t_ref):
    core = lax.axis_index("core")
    for half, refs in ((core, (own_ref, pair_ref)), (1 - core, (own_far_ref, pair_far_ref))):
        for k, ref in enumerate(refs):
            for j in range(8):
                for c in range(4):
                    t_ref[half * 4 + c, k, :, j * 128 : (j + 1) * 128] = ref[j, c]


def gather_amps(*parts):
    return pl.pallas_call(
        amps_kernel,
        out_shape=jax.ShapeDtypeStruct((NC, 2, 96, 1024), BF16),
        compiler_params=params(8),
        cost_estimate=cost(0, 7 * MIB),
    )(*parts)


def inner_kernel(t_ref, v_ref, out_ref, held_ref, sems):
    def copy(b):
        return pltpu.make_async_copy(v_ref.at[:, b], held_ref.at[b], sems.at[b])

    for b in range(4):
        copy(b).start()
    t = t_ref[...].reshape(NC * 192, 1024)
    for b in range(4):
        copy(b).wait()
        v = jnp.concatenate([held_ref[b, j] for j in range(8)], axis=-1)
        prod = lax.dot_general(t, v, (((1,), (1,)), ((), ())), preferred_element_type=F32)
        out_ref[:, b * 192 : (b + 1) * 192] = prod.astype(BF16).reshape(NC, 192, 512)


def inner_terms(t, v):
    return pl.pallas_call(
        inner_kernel,
        in_specs=[pl.BlockSpec(memory_space=pltpu.VMEM), pl.BlockSpec(memory_space=pl.ANY)],
        out_shape=jax.ShapeDtypeStruct((NC, 768, 512), BF16),
        scratch_shapes=[pltpu.VMEM((4, 8, 512, 128), BF16), pltpu.SemaphoreType.DMA((4,))],
        compiler_params=params(24),
        cost_estimate=cost(2 * 4 * 1536 * 1024 * 512, 13 * MIB),
    )(t, v)


def merge_kernel(mine0, mine1, far0, far1, out_ref):
    x = 2 * lax.axis_index("pair") + lax.axis_index("x_lo")
    low = lax.broadcasted_iota(jnp.int32, (256, 128), 1) < 64
    for n, (mine_ref, far_ref) in enumerate(((mine0, far0), (mine1, far1))):
        lanes = slice(n * 128, n * 128 + 128)
        for i in range(NC):
            c = 2 * lax.rem(x + i // 2, 4) + i % 2
            mine, far = mine_ref[i].astype(F32), far_ref[i].astype(F32)
            out_ref[c, :256, lanes] = jnp.where(low, mine, pltpu.roll(far, 64, 1)).astype(BF16)
            out_ref[c, 256:, lanes] = jnp.where(low, pltpu.roll(mine, 64, 1), far).astype(BF16)


def merge(mine, far):
    return pl.pallas_call(
        merge_kernel,
        out_shape=jax.ShapeDtypeStruct((NC, 512, 256), BF16),
        compiler_params=params(8),
        cost_estimate=cost(0, 4 * MIB),
    )(*mine, *far)


def ladder_kernel(s_ref, w_ref, own_ref, give_ref):
    lhs = jnp.concatenate([s_ref[c] for c in range(NC)], axis=1)
    total = jnp.dot(lhs, w_ref[...].reshape(NC * 512, 256), preferred_element_type=F32)
    total = total.reshape(4, 2, 96, 256)
    own_ref[...] = total[:, 0]
    give_ref[...] = total[:, 1].astype(BF16)


def ladder_part(inner, weights):
    return pl.pallas_call(
        ladder_kernel,
        out_shape=(jax.ShapeDtypeStruct((4, 96, 256), F32), jax.ShapeDtypeStruct((4, 96, 256), BF16)),
        compiler_params=params(12),
        cost_estimate=cost(2 * 768 * 4096 * 256, 8 * MIB),
    )(inner, weights)


def assemble_kernel(*refs):
    owns, gots, out_ref = refs[:4], refs[4:8], refs[8]
    z, pair, core = (lax.axis_index(a) for a in ("z", "pair", "core"))

    def place(mine, theirs, turn):
        for i, shift in enumerate(sum(SHIFTS, ())):
            lanes = pl.ds(pl.multiple_of(lax.rem(z + 8 + shift, 8) * 128, 128), 128)
            cols = slice(i % 2 * 128, i % 2 * 128 + 128)
            for b in range(4):
                for first, ref in ((mine, owns[i // 2]), (theirs, gots[i // 2])):
                    part = ref[b, :, cols].astype(F32)
                    out_ref[:, first + b, lanes] = pltpu.roll(part, 64, 1) if turn else part

    for k in range(2):
        for turn in range(2):

            @pl.when((pair == k) & (core == turn))
            def _():
                place(4 * k, 4 - 4 * k, turn)


def assemble(own, got):
    return pl.pallas_call(
        assemble_kernel,
        grid=(3,),
        in_specs=[pl.BlockSpec((4, 32, 256), lambda i: (0, i, 0))] * 8,
        out_specs=pl.BlockSpec((32, 8, 1024), lambda p: (p, 0, 0)),
        out_shape=jax.ShapeDtypeStruct((96, 8, 1024), F32),
        compiler_params=params(16),
        cost_estimate=cost(0, 6 * MIB),
    )(*own, *got)


def spread(w):
    y, x_lo, pair = (lax.axis_index(a) for a in ("y", "x_lo", "pair"))
    quarters = w.reshape(4, 2, 256, 128)
    keep = lax.dynamic_index_in_dim(quarters, 2 * pair, 0, False)
    give = lax.dynamic_index_in_dim(quarters, 2 * pair + 1, 0, False)
    got = send(give, dx=1, only=lambda x, y: x % 2 == 0 and y == 0)
    piece = jnp.where(x_lo == 0, keep, got)
    up, down, two = (send(piece, dy=d, only=lambda x, y: y == 0) for d in (1, -1, 2))
    piece = jnp.where(y == 0, piece, jnp.where(y == 1, up, jnp.where(y == 3, down, two)))
    rest = [send(piece, dx=-d) for d in (1, 2, 3)]
    return jnp.concatenate([piece, *rest], axis=0)


def per_device(vertex, amps):
    core = lax.axis_index("core")
    by_g = jnp.transpose(vertex, (2, 0, 1))
    w_source = window(by_g)
    w = spread(w_source)
    t = jnp.transpose(amps, (1, 0, 2))
    t = lax.dynamic_slice_in_dim(t, core * 4, 4, 0)
    t = lax.all_to_all(jnp.broadcast_to(t, (8, 4, 96, 128)), ("y", "x_lo"), 0, 0, tiled=True)
    t_pair = send(t, dx=2)
    v = vertex_rows(after(by_g, w_source))
    v = lax.all_to_all(after(v, t), ("y", "x_lo"), 0, 0, tiled=True)
    t = gather_amps(t, t_pair, send(t, dc=1), send(t_pair, dc=1))

    ups, downs = [w], [w]
    for _ in range(3):
        ups.append(send(ups[-1], dz=1))
        downs.append(send(downs[-1], dz=-1))
    opposite = jnp.concatenate([send(ups[-1][:4], dz=1), send(downs[-1][4:], dz=-1)], 0)
    weights = []
    for blocks in [(ups[i], downs[i]) for i in (1, 2, 3)] + [(w, opposite)]:
        weights.append(merge(blocks, [send(block, dc=1) for block in blocks]))

    inner = inner_terms(t, v)
    parts = [ladder_part(inner, weight) for weight in weights]
    return assemble([own for own, _ in parts], [send(give, dx=2) for _, give in parts])


def solution(mesh):
    fine = Mesh(mesh.devices.reshape(SIZES), AXES)
    return jax.shard_map(
        per_device,
        mesh=fine,
        in_specs=(P(("z", "core"), ("y", "x_lo"), None), P("pair", None, ("y", "x_lo"))),
        out_specs=P("pair", ("z", "core", "y", "x_lo"), None),
        check_vma=False,
    )
```

```python
import jax
import jax.numpy as jnp
import numpy as np
from jax import lax
from jax.experimental import pallas as pl
from jax.experimental.pallas import tpu as pltpu
from jax.sharding import Mesh, PartitionSpec as P

NC, NG = 8, 500
AXES = ("z", "core", "y", "x_lo", "pair")
SIZES = (8, 2, 4, 2, 2)
MIB = 1 << 20
F32, BF16 = jnp.float32, jnp.bfloat16
CHUNKS = ((0, 3), (3, 1))
SHIFTS = ((-1, 1), (-2, 2), (-3, 3), (0, 4))


def flat(x, y, z, c):
    x, y, z, c = x % 4, y % 4, z % 8, c % 2
    return ((z * 2 + c) * 8 + (y * 2 + x % 2)) * 2 + x // 2


def send(value, dx=0, dy=0, dz=0, dc=0, only=lambda x, y: True):
    pairs = [
        (flat(x, y, z, c), flat(x + dx, y + dy, z + dz, c + dc))
        for x in range(4)
        for y in range(4)
        for z in range(8)
        for c in range(2)
        if only(x, y)
    ]
    return lax.ppermute(value, AXES, pairs)


def after(value, *earlier):
    return lax.optimization_barrier((value, *earlier))[0]


def params(mib=24):
    return pltpu.CompilerParams(vmem_limit_bytes=mib * MIB)


def cost(flops, nbytes):
    return pl.CostEstimate(flops=flops, bytes_accessed=nbytes, transcendentals=0)


I, D = np.arange(2048) // 128, np.arange(2048) % 128
PICK = ((I[:, None] == np.arange(128) % 16) & (D[:, None] == np.arange(128) // 16)).astype(BF16)
R, K = np.arange(128), np.arange(256)
ROWS = np.stack(
    [
        (K[None] // 16 == R[:, None] % 16) & (K[None] % 16 == (8 * (R // 64) + 4 * k + (R // 16) % 4)[:, None])
        for k in range(2)
    ]
).astype(BF16)


def window_kernel(lo_ref, hi_ref, pick_ref, w_ref):
    for s in range(8):
        cols = []
        for i in range(16):
            hi = hi_ref[16 * s + i]
            if s == 7:
                hi = jnp.where(256 + 128 * pl.program_id(0) + 16 * s + i < NG, hi, 0)
            cols.append(jnp.concatenate([lo_ref[16 * s + i], hi], axis=0))
        picked = jnp.dot(jnp.concatenate(cols, axis=1), pick_ref[...], preferred_element_type=F32)
        w_ref[:, 16 * s : 16 * s + 16] = jnp.transpose(picked).astype(BF16).reshape(NC, 16, 128)


def window(by_g):
    return pl.pallas_call(
        window_kernel,
        grid=(2,),
        in_specs=[
            pl.BlockSpec((128, 64, 128), lambda u: (u, 0, 0)),
            pl.BlockSpec((128, 64, 128), lambda u: (2 + u, 0, 0)),
            pl.BlockSpec((2048, 128), lambda u: (0, 0)),
        ],
        out_specs=pl.BlockSpec((NC, 128, 128), lambda u: (0, u, 0)),
        out_shape=jax.ShapeDtypeStruct((NC, 256, 128), BF16),
        compiler_params=params(56),
        cost_estimate=cost(2 * 2048 * 2048 * 128, 9 * MIB),
    )(by_g, by_g, jnp.asarray(PICK))


def rows_kernel(x_ref, rows_ref, *v_refs):
    pair = lax.axis_index("pair")
    for s in range(16):
        x = x_ref[16 * s : 16 * s + 16]
        if s >= 14:
            g = lax.broadcasted_iota(jnp.int32, (16, 64, 128), 0) + (256 * pl.program_id(0) + 16 * s)
            x = jnp.where(g < NG, x, 0)
        for jj in range(4):
            picked = jnp.dot(
                rows_ref[pair], x[:, 16 * jj : 16 * jj + 16].reshape(256, 128), preferred_element_type=F32
            )
            picked = picked.astype(BF16).reshape(2, 4, 16, 128)
            for (first, count), v_ref in zip(CHUNKS, v_refs):
                v_ref[2 * jj : 2 * jj + 2, :, 16 * s : 16 * s + 16] = picked[:, first : first + count]


def vertex_rows(by_g):
    return pl.pallas_call(
        rows_kernel,
        grid=(2,),
        in_specs=[
            pl.BlockSpec((256, 64, 128), lambda u: (u, 0, 0)),
            pl.BlockSpec((2, 128, 256), lambda u: (0, 0, 0)),
        ],
        out_specs=[pl.BlockSpec((8, n, 256, 128), lambda u: (0, 0, u, 0)) for _, n in CHUNKS],
        out_shape=[jax.ShapeDtypeStruct((8, n, 512, 128), BF16) for _, n in CHUNKS],
        compiler_params=params(56),
        cost_estimate=cost(2 * 2048 * 2048 * 128, 13 * MIB),
    )(by_g, jnp.asarray(ROWS))


def amps_kernel(own_ref, pair_ref, own_far_ref, pair_far_ref, t_ref):
    core = lax.axis_index("core")
    for half, refs in ((core, (own_ref, pair_ref)), (1 - core, (own_far_ref, pair_far_ref))):
        for k, ref in enumerate(refs):
            for j in range(8):
                for c in range(4):
                    t_ref[half * 4 + c, k, :, j * 128 : (j + 1) * 128] = ref[j, c]


def gather_amps(*parts):
    return pl.pallas_call(
        amps_kernel,
        out_shape=jax.ShapeDtypeStruct((NC, 2, 96, 1024), BF16),
        compiler_params=params(8),
        cost_estimate=cost(0, 7 * MIB),
    )(*parts)


def inner_kernel(t_ref, v_ref, out_ref, held_ref, sems):
    rows = v_ref.shape[1]

    def copy(b):
        return pltpu.make_async_copy(v_ref.at[:, b], held_ref.at[b], sems.at[b])

    for b in range(rows):
        copy(b).start()
    t = t_ref[...].reshape(NC * 192, 1024)
    for b in range(rows):
        copy(b).wait()
        v = jnp.concatenate([held_ref[b, j] for j in range(8)], axis=-1)
        prod = lax.dot_general(t, v, (((1,), (1,)), ((), ())), preferred_element_type=F32)
        out_ref[:, b * 192 : (b + 1) * 192] = prod.astype(BF16).reshape(NC, 192, 512)


def inner_terms(t, v):
    rows = v.shape[1]
    return pl.pallas_call(
        inner_kernel,
        in_specs=[pl.BlockSpec(memory_space=pltpu.VMEM), pl.BlockSpec(memory_space=pl.ANY)],
        out_shape=jax.ShapeDtypeStruct((NC, rows * 192, 512), BF16),
        scratch_shapes=[pltpu.VMEM((rows, 8, 512, 128), BF16), pltpu.SemaphoreType.DMA((rows,))],
        compiler_params=params(24),
        cost_estimate=cost(2 * rows * 1536 * 1024 * 512, 8 * MIB),
    )(t, v)


def merge_kernel(mine0, mine1, far0, far1, out_ref):
    x = 2 * lax.axis_index("pair") + lax.axis_index("x_lo")
    low = lax.broadcasted_iota(jnp.int32, (256, 128), 1) < 64
    for n, (mine_ref, far_ref) in enumerate(((mine0, far0), (mine1, far1))):
        lanes = slice(n * 128, n * 128 + 128)
        for i in range(NC):
            c = i + 4 * (x // 2) - 8 * (x // 2) * (i // 4)
            mine, far = mine_ref[i].astype(F32), far_ref[i].astype(F32)
            out_ref[c, :256, lanes] = jnp.where(low, mine, pltpu.roll(far, 64, 1)).astype(BF16)
            out_ref[c, 256:, lanes] = jnp.where(low, pltpu.roll(mine, 64, 1), far).astype(BF16)


def merge(mine, far):
    return pl.pallas_call(
        merge_kernel,
        out_shape=jax.ShapeDtypeStruct((NC, 512, 256), BF16),
        compiler_params=params(8),
        cost_estimate=cost(0, 4 * MIB),
    )(*mine, *far)


def ladder_kernel(s_ref, w_ref, own_ref, give_ref):
    lhs = jnp.concatenate([s_ref[c] for c in range(NC)], axis=1)
    total = jnp.dot(lhs, w_ref[...].reshape(NC * 512, 256), preferred_element_type=F32)
    total = total.reshape(-1, 2, 96, 256)
    own_ref[...] = total[:, 0]
    give_ref[...] = total[:, 1].astype(BF16)


def ladder_part(inner, weights):
    rows = inner.shape[1] // 192
    return pl.pallas_call(
        ladder_kernel,
        out_shape=(jax.ShapeDtypeStruct((rows, 96, 256), F32), jax.ShapeDtypeStruct((rows, 96, 256), BF16)),
        compiler_params=params(12),
        cost_estimate=cost(2 * rows * 192 * 4096 * 256, 8 * MIB),
    )(inner, weights)


def assemble_kernel(*refs):
    n = 4 * len(CHUNKS)
    owns, gots, out_ref = refs[:n], refs[n : 2 * n], refs[2 * n]
    z, pair, core = (lax.axis_index(a) for a in ("z", "pair", "core"))

    def place(mine, theirs, turn):
        for i, shift in enumerate(sum(SHIFTS, ())):
            lanes = pl.ds(pl.multiple_of(lax.rem(z + 8 + shift, 8) * 128, 128), 128)
            cols = slice(i % 2 * 128, i % 2 * 128 + 128)
            for m, (start, count) in enumerate(CHUNKS):
                for b in range(count):
                    for first, ref in ((mine, owns[4 * m + i // 2]), (theirs, gots[4 * m + i // 2])):
                        part = ref[b, :, cols].astype(F32)
                        out_ref[:, first + start + b, lanes] = pltpu.roll(part, 64, 1) if turn else part

    for k in range(2):
        for turn in range(2):

            @pl.when((pair == k) & (core == turn))
            def _():
                place(4 * k, 4 - 4 * k, turn)


def assemble(own, got):
    pieces = [*own, *got]
    return pl.pallas_call(
        assemble_kernel,
        grid=(3,),
        in_specs=[pl.BlockSpec((p.shape[0], 32, 256), lambda i: (0, i, 0)) for p in pieces],
        out_specs=pl.BlockSpec((32, 8, 1024), lambda p: (p, 0, 0)),
        out_shape=jax.ShapeDtypeStruct((96, 8, 1024), F32),
        compiler_params=params(16),
        cost_estimate=cost(0, 6 * MIB),
    )(*pieces)


def spread_over_y(w):
    y, pair = lax.axis_index("y"), lax.axis_index("pair")
    half = lax.dynamic_slice_in_dim(w, 4 * pair, 4, 0)
    up, down, two = (send(half, dy=d, only=lambda x, y: x % 2 == 0 and y == 0) for d in (1, -1, 2))
    return jnp.where(y == 0, half, jnp.where(y == 1, up, jnp.where(y == 3, down, two)))


def spread_over_x(half):
    x_lo = lax.axis_index("x_lo")
    even = lambda x, y: x % 2 == 0
    left, right, other = (send(half, dx=d, only=even) for d in (1, -1, 2))
    return jnp.concatenate([jnp.where(x_lo == 0, half, left), jnp.where(x_lo == 0, other, right)], axis=0)


def per_device(vertex, amps):
    core = lax.axis_index("core")
    by_g = jnp.transpose(vertex, (2, 0, 1))
    w_source = window(by_g)
    half = spread_over_y(w_source)

    t = jnp.transpose(amps, (1, 0, 2))
    t = lax.dynamic_slice_in_dim(t, core * 4, 4, 0)
    t = after(jnp.broadcast_to(t, (8, 4, 96, 128)), w_source)
    t = lax.all_to_all(t, ("y", "x_lo"), 0, 0, tiled=True)

    v0, v1 = vertex_rows(after(by_g, w_source))
    v0, half = lax.optimization_barrier((after(v0, t), half))
    v0 = lax.all_to_all(v0, ("y", "x_lo"), 0, 0, tiled=True)
    v1 = lax.all_to_all(after(v1, v0), ("y", "x_lo"), 0, 0, tiled=True)

    w = spread_over_x(half)
    t_pair = send(t, dx=2)
    t = gather_amps(t, t_pair, send(t, dc=1), send(t_pair, dc=1))

    ups, downs = [w], [w]
    for _ in range(3):
        ups.append(send(ups[-1], dz=1))
        downs.append(send(downs[-1], dz=-1))
    last = after((ups[-1][:4], downs[-1][4:]), v0)
    opposite = jnp.concatenate([send(last[0], dz=1), send(last[1], dz=-1)], 0)
    weights = []
    for blocks in [(ups[i], downs[i]) for i in (1, 2, 3)] + [(w, opposite)]:
        weights.append(merge(blocks, [send(block, dc=1) for block in blocks]))

    own, got = [], []
    for v in (v0, v1):
        inner = inner_terms(t, v)
        for weight in weights:
            mine, give = ladder_part(inner, weight)
            own.append(mine)
            got.append(send(give, dx=2))
    return assemble(own, got)


def solution(mesh):
    fine = Mesh(mesh.devices.reshape(SIZES), AXES)
    return jax.shard_map(
        per_device,
        mesh=fine,
        in_specs=(P(("z", "core"), ("y", "x_lo"), None), P("pair", None, ("y", "x_lo"))),
        out_specs=P("pair", ("z", "core", "y", "x_lo"), None),
        check_vma=False,
    )
```

```python
import jax
import jax.numpy as jnp
import numpy as np
from jax import lax
from jax.experimental import pallas as pl
from jax.experimental.pallas import tpu as pltpu
from jax.sharding import Mesh, PartitionSpec as P

NC, NG = 8, 500
AXES = ("z", "core", "y", "x_lo", "pair")
SIZES = (8, 2, 4, 2, 2)
MIB = 1 << 20
F32, BF16 = jnp.float32, jnp.bfloat16
CHUNKS = ((0, 3), (3, 1))
SHIFTS = ((-1, 1), (-2, 2), (-3, 3), (0, 4))


def flat(x, y, z, c):
    x, y, z, c = x % 4, y % 4, z % 8, c % 2
    return ((z * 2 + c) * 8 + (y * 2 + x % 2)) * 2 + x // 2


def send(value, dx=0, dy=0, dz=0, dc=0, only=lambda x, y: True):
    pairs = [
        (flat(x, y, z, c), flat(x + dx, y + dy, z + dz, c + dc))
        for x in range(4)
        for y in range(4)
        for z in range(8)
        for c in range(2)
        if only(x, y)
    ]
    return lax.ppermute(value, AXES, pairs)


def over_y(value):
    return lax.all_to_all(value, "y", 0, 0, tiled=True)


def after(value, *earlier):
    return lax.optimization_barrier((value, *earlier))[0]


def params(mib=24):
    return pltpu.CompilerParams(vmem_limit_bytes=mib * MIB)


def cost(flops, nbytes):
    return pl.CostEstimate(flops=flops, bytes_accessed=nbytes, transcendentals=0)


I, D = np.arange(2048) // 128, np.arange(2048) % 128
PICK = ((I[:, None] == np.arange(128) % 16) & (D[:, None] == np.arange(128) // 16)).astype(BF16)
R, K = np.arange(128), np.arange(256)


def chosen_rows(x):
    first = [8 * (o % 4 % 2) + 4 * (o % 4 // 2) for o in (x, x + 1, x + 3)]
    rows = np.array([first[0] + b for b in range(4)] + [first[1], first[1] + 1, first[2] + 2, first[2] + 3])
    return (K[None] // 16 == R[:, None] % 16) & (K[None] % 16 == rows[R // 16][:, None])


ROWS = np.stack([chosen_rows(x) for x in range(4)]).astype(BF16)


def window_kernel(lo_ref, hi_ref, pick_ref, w_ref):
    for s in range(8):
        cols = []
        for i in range(16):
            hi = hi_ref[16 * s + i]
            if s == 7:
                hi = jnp.where(256 + 128 * pl.program_id(0) + 16 * s + i < NG, hi, 0)
            cols.append(jnp.concatenate([lo_ref[16 * s + i], hi], axis=0))
        picked = jnp.dot(jnp.concatenate(cols, axis=1), pick_ref[...], preferred_element_type=F32)
        w_ref[:, 16 * s : 16 * s + 16] = jnp.transpose(picked).astype(BF16).reshape(NC, 16, 128)


def window(by_g):
    return pl.pallas_call(
        window_kernel,
        grid=(2,),
        in_specs=[
            pl.BlockSpec((128, 64, 128), lambda u: (u, 0, 0)),
            pl.BlockSpec((128, 64, 128), lambda u: (2 + u, 0, 0)),
            pl.BlockSpec((2048, 128), lambda u: (0, 0)),
        ],
        out_specs=pl.BlockSpec((NC, 128, 128), lambda u: (0, u, 0)),
        out_shape=jax.ShapeDtypeStruct((NC, 256, 128), BF16),
        compiler_params=params(56),
        cost_estimate=cost(2 * 2048 * 2048 * 128, 9 * MIB),
    )(by_g, by_g, jnp.asarray(PICK))


PARTS = ((0, 3), (3, 1), (4, 2), (6, 1), (7, 1))


def rows_kernel(x_ref, rows_ref, *v_refs):
    x = 2 * lax.axis_index("pair") + lax.axis_index("x_lo")
    for s in range(16):
        block = x_ref[16 * s : 16 * s + 16]
        if s >= 14:
            g = lax.broadcasted_iota(jnp.int32, (16, 64, 128), 0) + (256 * pl.program_id(0) + 16 * s)
            block = jnp.where(g < NG, block, 0)
        for y in range(4):
            picked = jnp.dot(
                rows_ref[x], block[:, 16 * y : 16 * y + 16].reshape(256, 128), preferred_element_type=F32
            )
            picked = picked.astype(BF16).reshape(8, 16, 128)
            for (first, count), v_ref in zip(PARTS, v_refs):
                v_ref[y, :, 16 * s : 16 * s + 16] = picked[first : first + count]


def vertex_rows(by_g):
    return pl.pallas_call(
        rows_kernel,
        grid=(2,),
        in_specs=[
            pl.BlockSpec((256, 64, 128), lambda u: (u, 0, 0)),
            pl.BlockSpec((4, 128, 256), lambda u: (0, 0, 0)),
        ],
        out_specs=[pl.BlockSpec((4, n, 256, 128), lambda u: (0, 0, u, 0)) for _, n in PARTS],
        out_shape=[jax.ShapeDtypeStruct((4, n, 512, 128), BF16) for _, n in PARTS],
        compiler_params=params(56),
        cost_estimate=cost(2 * 2048 * 2048 * 128, 13 * MIB),
    )(by_g, jnp.asarray(ROWS))


def amps_kernel(mine_ref, far_ref, t_ref):
    core, x_lo = lax.axis_index("core"), lax.axis_index("x_lo")
    for half, ref in ((core, mine_ref), (1 - core, far_ref)):
        for n, (side, k) in enumerate(((0, 0), (1, x_lo), (1, 1 - x_lo), (0, 1))):
            for y in range(4):
                lanes = slice((2 * y + side) * 128, (2 * y + side) * 128 + 128)
                for c in range(4):
                    t_ref[half * 4 + c, k, :, lanes] = ref[n, y, c]


def gather_amps(mine, far):
    return pl.pallas_call(
        amps_kernel,
        out_shape=jax.ShapeDtypeStruct((NC, 2, 96, 1024), BF16),
        compiler_params=params(8),
        cost_estimate=cost(0, 7 * MIB),
    )(mine, far)


def inner_kernel(t_ref, own_ref, other_ref, out_ref, held_ref, sems):
    rows = own_ref.shape[1]

    def copies(b):
        return [
            pltpu.make_async_copy(ref.at[:, b], held_ref.at[b, n], sems.at[b, n])
            for n, ref in enumerate((own_ref, other_ref))
        ]

    for b in range(rows):
        for copy in copies(b):
            copy.start()
    t = t_ref[...].reshape(NC * 192, 1024)
    for b in range(rows):
        for copy in copies(b):
            copy.wait()
        v = jnp.concatenate([held_ref[b, n, y] for y in range(4) for n in range(2)], axis=-1)
        prod = lax.dot_general(t, v, (((1,), (1,)), ((), ())), preferred_element_type=F32)
        out_ref[:, b * 192 : (b + 1) * 192] = prod.astype(BF16).reshape(NC, 192, 512)


def inner_terms(t, own, other):
    rows = own.shape[1]
    return pl.pallas_call(
        inner_kernel,
        in_specs=[pl.BlockSpec(memory_space=pltpu.VMEM)] + [pl.BlockSpec(memory_space=pl.ANY)] * 2,
        out_shape=jax.ShapeDtypeStruct((NC, rows * 192, 512), BF16),
        scratch_shapes=[pltpu.VMEM((rows, 2, 4, 512, 128), BF16), pltpu.SemaphoreType.DMA((rows, 2))],
        compiler_params=params(20),
        cost_estimate=cost(2 * rows * 1536 * 1024 * 512, 8 * MIB),
    )(t, own, other)


def merge_kernel(mine0, mine1, far0, far1, out_ref):
    x = 2 * lax.axis_index("pair") + lax.axis_index("x_lo")
    low = lax.broadcasted_iota(jnp.int32, (256, 128), 1) < 64
    for n, (mine_ref, far_ref) in enumerate(((mine0, far0), (mine1, far1))):
        lanes = slice(n * 128, n * 128 + 128)
        for i in range(NC):
            c = i + 4 * (x // 2) - 8 * (x // 2) * (i // 4)
            mine, far = mine_ref[i].astype(F32), far_ref[i].astype(F32)
            out_ref[c, :256, lanes] = jnp.where(low, mine, pltpu.roll(far, 64, 1)).astype(BF16)
            out_ref[c, 256:, lanes] = jnp.where(low, pltpu.roll(mine, 64, 1), far).astype(BF16)


def merge(mine, far):
    return pl.pallas_call(
        merge_kernel,
        out_shape=jax.ShapeDtypeStruct((NC, 512, 256), BF16),
        compiler_params=params(8),
        cost_estimate=cost(0, 4 * MIB),
    )(*mine, *far)


def ladder_kernel(s_ref, w_ref, own_ref, give_ref):
    lhs = jnp.concatenate([s_ref[c] for c in range(NC)], axis=1)
    total = jnp.dot(lhs, w_ref[...].reshape(NC * 512, 256), preferred_element_type=F32)
    total = total.reshape(-1, 2, 96, 256)
    own_ref[...] = total[:, 0]
    give_ref[...] = total[:, 1].astype(BF16)


def ladder_part(inner, weights):
    rows = inner.shape[1] // 192
    return pl.pallas_call(
        ladder_kernel,
        out_shape=(jax.ShapeDtypeStruct((rows, 96, 256), F32), jax.ShapeDtypeStruct((rows, 96, 256), BF16)),
        compiler_params=params(12),
        cost_estimate=cost(2 * rows * 192 * 4096 * 256, 8 * MIB),
    )(inner, weights)


def assemble_kernel(*refs):
    n = 4 * len(CHUNKS)
    owns, gots, out_ref = refs[:n], refs[n : 2 * n], refs[2 * n]
    z, pair, core = (lax.axis_index(a) for a in ("z", "pair", "core"))
    first_p = pl.multiple_of(32 * pl.program_id(0), 32)

    def place(mine, theirs, turn):
        for i, shift in enumerate(sum(SHIFTS, ())):
            lanes = pl.ds(pl.multiple_of(lax.rem(z + 8 + shift, 8) * 128, 128), 128)
            cols = slice(i % 2 * 128, i % 2 * 128 + 128)
            for m, (start, count) in enumerate(CHUNKS):
                for b in range(count):
                    for first, ref in ((mine, owns[4 * m + i // 2]), (theirs, gots[4 * m + i // 2])):
                        part = ref[b, pl.ds(first_p, 32), cols].astype(F32)
                        out_ref[:, first + start + b, lanes] = pltpu.roll(part, 64, 1) if turn else part

    for k in range(2):
        for turn in range(2):

            @pl.when((pair == k) & (core == turn))
            def _():
                place(4 * k, 4 - 4 * k, turn)


def assemble(own, got):
    pieces = [*own, *got]
    return pl.pallas_call(
        assemble_kernel,
        grid=(3,),
        in_specs=[pl.BlockSpec(memory_space=pltpu.VMEM)] * len(pieces),
        out_specs=pl.BlockSpec((32, 8, 1024), lambda p: (p, 0, 0)),
        out_shape=jax.ShapeDtypeStruct((96, 8, 1024), F32),
        compiler_params=params(16),
        cost_estimate=cost(0, 6 * MIB),
    )(*pieces)


def spread_over_y(w):
    y, pair = lax.axis_index("y"), lax.axis_index("pair")
    half = lax.dynamic_slice_in_dim(w, 4 * pair, 4, 0)
    up, down, two = (send(half, dy=d, only=lambda x, y: x % 2 == 0 and y == 0) for d in (1, -1, 2))
    return jnp.where(y == 0, half, jnp.where(y == 1, up, jnp.where(y == 3, down, two)))


def spread_over_x(half):
    x_lo = lax.axis_index("x_lo")
    even = lambda x, y: x % 2 == 0
    left, right, other = (send(half, dx=d, only=even) for d in (1, -1, 2))
    return jnp.concatenate([jnp.where(x_lo == 0, half, left), jnp.where(x_lo == 0, other, right)], axis=0)


def per_device(vertex, amps):
    core = lax.axis_index("core")
    by_g = jnp.transpose(vertex, (2, 0, 1))
    w_source = window(by_g)
    half = spread_over_y(w_source)

    t = jnp.transpose(amps, (1, 0, 2))
    t = lax.dynamic_slice_in_dim(t, core * 4, 4, 0)
    t = over_y(jnp.broadcast_to(t, (4, 4, 96, 128)))

    own_a, own_b, right, left_a, left_b = vertex_rows(after(by_g, w_source))
    own_a, half = lax.optimization_barrier((after(own_a, t), half))
    own_a = over_y(own_a)
    w = spread_over_x(half)

    other_a = jnp.concatenate([send(right, dx=1), send(left_a, dx=-1)], axis=1)
    other_b = send(left_b, dx=-1)
    other_a = over_y(after(other_a, own_a))
    both_b = over_y(after(jnp.concatenate([own_b, other_b], axis=1), other_a))

    t = jnp.stack([t, send(t, dx=-1), send(t, dx=1), send(t, dx=2)])
    t = gather_amps(t, send(t, dc=1))

    ups, downs = [w], [w]
    for _ in range(3):
        ups.append(send(ups[-1], dz=1))
        downs.append(send(downs[-1], dz=-1))
    last = (ups[-1][:4], downs[-1][4:])
    opposite = jnp.concatenate([send(last[0], dz=1), send(last[1], dz=-1)], 0)
    weights = []
    for blocks in [(ups[i], downs[i]) for i in (1, 2, 3)] + [(w, opposite)]:
        weights.append(merge(blocks, [send(block, dc=1) for block in blocks]))

    own, got = [], []
    for block, other in ((own_a, other_a), (both_b[:, :1], both_b[:, 1:])):
        inner = inner_terms(t, block, other)
        for weight in weights:
            mine, give = ladder_part(inner, weight)
            own.append(mine)
            got.append(send(give, dx=2))
    return assemble(own, got)


def solution(mesh):
    fine = Mesh(mesh.devices.reshape(SIZES), AXES)
    return jax.shard_map(
        per_device,
        mesh=fine,
        in_specs=(P(("z", "core"), ("y", "x_lo"), None), P("pair", None, ("y", "x_lo"))),
        out_specs=P("pair", ("z", "core", "y", "x_lo"), None),
        check_vma=False,
    )
```

```python
import jax
import jax.numpy as jnp
import numpy as np
from jax import lax
from jax.experimental import pallas as pl
from jax.experimental.pallas import tpu as pltpu
from jax.sharding import Mesh, PartitionSpec as P

NC, NG = 8, 500
AXES = ("z", "core", "y", "x_lo", "pair")
SIZES = (8, 2, 4, 2, 2)
MIB = 1 << 20
F32, BF16 = jnp.float32, jnp.bfloat16
SHIFTS = ((-1, 1), (-2, 2), (-3, 3), (0, 4))


def flat(x, y, z, c):
    x, y, z, c = x % 4, y % 4, z % 8, c % 2
    return ((z * 2 + c) * 8 + (y * 2 + x % 2)) * 2 + x // 2


def send(value, dx=0, dy=0, dz=0, dc=0, only=lambda x, y: True):
    pairs = [
        (flat(x, y, z, c), flat(x + dx, y + dy, z + dz, c + dc))
        for x in range(4)
        for y in range(4)
        for z in range(8)
        for c in range(2)
        if only(x, y)
    ]
    return lax.ppermute(value, AXES, pairs)


def over_y(value):
    return lax.all_to_all(value, "y", 0, 0, tiled=True)


def after(value, *earlier):
    return lax.optimization_barrier((value, *earlier))[0]


def params(mib=24):
    return pltpu.CompilerParams(vmem_limit_bytes=mib * MIB)


def cost(flops, nbytes):
    return pl.CostEstimate(flops=flops, bytes_accessed=nbytes, transcendentals=0)


I, D = np.arange(2048) // 128, np.arange(2048) % 128
PICK = ((I[:, None] == np.arange(128) % 16) & (D[:, None] == np.arange(128) // 16)).astype(BF16)
R, K = np.arange(128), np.arange(256)


def chosen_rows(x):
    first = [8 * (o % 4 % 2) + 4 * (o % 4 // 2) for o in (x, x + 1, x + 3)]
    rows = np.array([first[0] + b for b in range(4)] + [first[1], first[1] + 1, first[2] + 2, first[2] + 3])
    return (K[None] // 16 == R[:, None] % 16) & (K[None] % 16 == rows[R // 16][:, None])


ROWS = np.stack([chosen_rows(x) for x in range(4)]).astype(BF16)


def window_kernel(lo_ref, hi_ref, pick_ref, w_ref):
    for s in range(8):
        cols = []
        for i in range(16):
            hi = hi_ref[16 * s + i]
            if s == 7:
                hi = jnp.where(256 + 128 * pl.program_id(0) + 16 * s + i < NG, hi, 0)
            cols.append(jnp.concatenate([lo_ref[16 * s + i], hi], axis=0))
        picked = jnp.dot(jnp.concatenate(cols, axis=1), pick_ref[...], preferred_element_type=F32)
        w_ref[:, 16 * s : 16 * s + 16] = jnp.transpose(picked).astype(BF16).reshape(NC, 16, 128)


def window(by_g):
    return pl.pallas_call(
        window_kernel,
        grid=(2,),
        in_specs=[
            pl.BlockSpec((128, 64, 128), lambda u: (u, 0, 0)),
            pl.BlockSpec((128, 64, 128), lambda u: (2 + u, 0, 0)),
            pl.BlockSpec((2048, 128), lambda u: (0, 0)),
        ],
        out_specs=pl.BlockSpec((NC, 128, 128), lambda u: (0, u, 0)),
        out_shape=jax.ShapeDtypeStruct((NC, 256, 128), BF16),
        compiler_params=params(56),
        cost_estimate=cost(2 * 2048 * 2048 * 128, 9 * MIB),
    )(by_g, by_g, jnp.asarray(PICK))


PARTS = ((0, 2), (2, 2), (4, 2), (6, 2))


def rows_kernel(x_ref, rows_ref, *v_refs):
    x = 2 * lax.axis_index("pair") + lax.axis_index("x_lo")
    for s in range(16):
        block = x_ref[16 * s : 16 * s + 16]
        if s >= 14:
            g = lax.broadcasted_iota(jnp.int32, (16, 64, 128), 0) + (256 * pl.program_id(0) + 16 * s)
            block = jnp.where(g < NG, block, 0)
        for y in range(4):
            picked = jnp.dot(
                rows_ref[x], block[:, 16 * y : 16 * y + 16].reshape(256, 128), preferred_element_type=F32
            )
            picked = picked.astype(BF16).reshape(8, 16, 128)
            for (first, count), v_ref in zip(PARTS, v_refs):
                v_ref[y, :, 16 * s : 16 * s + 16] = picked[first : first + count]


def vertex_rows(by_g):
    return pl.pallas_call(
        rows_kernel,
        grid=(2,),
        in_specs=[
            pl.BlockSpec((256, 64, 128), lambda u: (u, 0, 0)),
            pl.BlockSpec((4, 128, 256), lambda u: (0, 0, 0)),
        ],
        out_specs=[pl.BlockSpec((4, n, 256, 128), lambda u: (0, 0, u, 0)) for _, n in PARTS],
        out_shape=[jax.ShapeDtypeStruct((4, n, 512, 128), BF16) for _, n in PARTS],
        compiler_params=params(56),
        cost_estimate=cost(2 * 2048 * 2048 * 128, 13 * MIB),
    )(by_g, jnp.asarray(ROWS))


def amps_kernel(*refs):
    t_ref = refs[4]
    x_lo = lax.axis_index("x_lo")
    for ref, (side, k) in zip(refs, ((0, 0), (1, x_lo), (1, 1 - x_lo), (0, 1))):
        for y in range(4):
            lanes = slice((2 * y + side) * 128, (2 * y + side) * 128 + 128)
            for c in range(NC):
                t_ref[c, k, :, lanes] = ref[y, c]


def gather_amps(*parts):
    return pl.pallas_call(
        amps_kernel,
        out_shape=jax.ShapeDtypeStruct((NC, 2, 96, 1024), BF16),
        compiler_params=params(8),
        cost_estimate=cost(0, 7 * MIB),
    )(*parts)


def inner_kernel(t_ref, v_ref, out_ref, held_ref, sems):
    def copies(b):
        return [pltpu.make_async_copy(v_ref.at[:, 2 * n + b], held_ref.at[b, n], sems.at[b, n]) for n in range(2)]

    for b in range(2):
        for copy in copies(b):
            copy.start()
    t = t_ref[...].reshape(NC * 192, 1024)
    for b in range(2):
        for copy in copies(b):
            copy.wait()
        v = jnp.concatenate([held_ref[b, n, y] for y in range(4) for n in range(2)], axis=-1)
        prod = lax.dot_general(t, v, (((1,), (1,)), ((), ())), preferred_element_type=F32)
        out_ref[:, b * 192 : (b + 1) * 192] = prod.astype(BF16).reshape(NC, 192, 512)


def inner_terms(t, v):
    return pl.pallas_call(
        inner_kernel,
        in_specs=[pl.BlockSpec(memory_space=pltpu.VMEM), pl.BlockSpec(memory_space=pl.ANY)],
        out_shape=jax.ShapeDtypeStruct((NC, 2 * 192, 512), BF16),
        scratch_shapes=[pltpu.VMEM((2, 2, 4, 512, 128), BF16), pltpu.SemaphoreType.DMA((2, 2))],
        compiler_params=params(20),
        cost_estimate=cost(2 * 2 * 1536 * 1024 * 512, 8 * MIB),
    )(t, v)


def merge_kernel(mine0, mine1, far0, far1, out_ref):
    x = 2 * lax.axis_index("pair") + lax.axis_index("x_lo")
    low = lax.broadcasted_iota(jnp.int32, (256, 128), 1) < 64
    for n, (mine_ref, far_ref) in enumerate(((mine0, far0), (mine1, far1))):
        lanes = slice(n * 128, n * 128 + 128)
        for i in range(NC):
            c = i + 4 * (x // 2) - 8 * (x // 2) * (i // 4)
            mine, far = mine_ref[i].astype(F32), far_ref[i].astype(F32)
            out_ref[c, :256, lanes] = jnp.where(low, mine, pltpu.roll(far, 64, 1)).astype(BF16)
            out_ref[c, 256:, lanes] = jnp.where(low, pltpu.roll(mine, 64, 1), far).astype(BF16)


def merge(mine, far):
    return pl.pallas_call(
        merge_kernel,
        out_shape=jax.ShapeDtypeStruct((NC, 512, 256), BF16),
        compiler_params=params(8),
        cost_estimate=cost(0, 4 * MIB),
    )(*mine, *far)


def ladder_kernel(n_inner, *refs):
    inner_refs, weight_refs, (own_ref, give_ref) = refs[:n_inner], refs[n_inner:-2], refs[-2:]
    for n, w_ref in enumerate(weight_refs):
        weight = w_ref[...].reshape(NC * 512, 256)
        for m, s_ref in enumerate(inner_refs):
            lhs = jnp.concatenate([s_ref[c] for c in range(NC)], axis=1)
            total = jnp.dot(lhs, weight, preferred_element_type=F32).reshape(2, 2, 96, 256)
            own_ref[2 * m : 2 * m + 2, :, n * 256 : n * 256 + 256] = total[:, 0]
            give_ref[2 * m : 2 * m + 2, :, n * 256 : n * 256 + 256] = total[:, 1].astype(BF16)


def ladder_part(inner, weights):
    rows, cols = 2 * len(inner), 256 * len(weights)

    def kernel(*refs):
        ladder_kernel(len(inner), *refs)

    return pl.pallas_call(
        kernel,
        out_shape=(jax.ShapeDtypeStruct((rows, 96, cols), F32), jax.ShapeDtypeStruct((rows, 96, cols), BF16)),
        compiler_params=params(12),
        cost_estimate=cost(2 * rows * 192 * 4096 * cols, 8 * MIB),
    )(*inner, *weights)


P_STEP = 48
PIECES = ((0, 2, 0, 6), (2, 2, 0, 6), (0, 4, 6, 2))


def assemble_kernel(*refs):
    owns, gots, (out_ref, held_ref) = refs[:3], refs[3:6], refs[6:]
    z, pair, core = (lax.axis_index(a) for a in ("z", "pair", "core"))
    shifts = sum(SHIFTS, ())

    def place(mine, theirs, turn):
        for (row, rows, block, blocks), own_ref, got_ref in zip(PIECES, owns, gots):
            for i in range(blocks):
                for b in range(rows):
                    for first, ref in ((mine, own_ref), (theirs, got_ref)):
                        part = ref[b, :, i * 128 : i * 128 + 128].astype(F32)
                        part = pltpu.roll(part, 64, 1) if turn else part
                        at = (first + row + b) * P_STEP
                        held_ref[block + i, at : at + P_STEP] = part

    for k in range(2):
        for turn in range(2):

            @pl.when((pair == k) & (core == turn))
            def _():
                place(4 * k, 4 - 4 * k, turn)

    for i, shift in enumerate(shifts):
        lanes = pl.ds(pl.multiple_of(lax.rem(z + 8 + shift, 8) * 128, 128), 128)
        for p in range(P_STEP):
            out_ref[p, :, lanes] = held_ref[i, pl.ds(p, 8, stride=P_STEP), :]


def assemble(own, got):
    pieces = [*own, *got]
    return pl.pallas_call(
        assemble_kernel,
        grid=(96 // P_STEP,),
        in_specs=[pl.BlockSpec((p.shape[0], P_STEP, p.shape[2]), lambda i: (0, i, 0)) for p in pieces],
        out_specs=pl.BlockSpec((P_STEP, 8, 1024), lambda p: (p, 0, 0)),
        out_shape=jax.ShapeDtypeStruct((96, 8, 1024), F32),
        scratch_shapes=[pltpu.VMEM((8, 8 * P_STEP, 128), F32)],
        compiler_params=params(16),
        cost_estimate=cost(0, 6 * MIB),
    )(*pieces)


def spread_over_y(w):
    y, pair = lax.axis_index("y"), lax.axis_index("pair")
    half = lax.dynamic_slice_in_dim(w, 4 * pair, 4, 0)
    up, down, two = (send(half, dy=d, only=lambda x, y: x % 2 == 0 and y == 0) for d in (1, -1, 2))
    return jnp.where(y == 0, half, jnp.where(y == 1, up, jnp.where(y == 3, down, two)))


def spread_over_x(half):
    x_lo = lax.axis_index("x_lo")
    even = lambda x, y: x % 2 == 0
    left, right, other = (send(half, dx=d, only=even) for d in (1, -1, 2))
    return jnp.concatenate([jnp.where(x_lo == 0, half, left), jnp.where(x_lo == 0, other, right)], axis=0)


def per_device(vertex, amps):
    by_g = jnp.transpose(vertex, (2, 0, 1))
    w_source = window(by_g)
    half = spread_over_y(w_source)

    t = after(jnp.broadcast_to(jnp.transpose(amps, (1, 0, 2)), (4, NC, 96, 128)), w_source)
    t = over_y(t)

    own_a, own_b, right, left = vertex_rows(after(by_g, w_source))
    right, left = send(right, dx=1), send(left, dx=-1)
    w = spread_over_x(after(half, right, left))
    v_a = jnp.concatenate([own_a, right], axis=1)
    v_b = jnp.concatenate([own_b, left], axis=1)
    v_a = over_y(after(v_a, t, left))
    v_b = over_y(after(v_b, v_a))

    ups, downs = [w], [w]
    for wait in (w, w, v_a):
        ups.append(send(after(ups[-1], wait), dz=1))
        downs.append(send(after(downs[-1], wait), dz=-1))

    t = after(t, w)
    t = gather_amps(t, *after((send(t, dx=-1), send(t, dx=1), send(t, dx=2)), v_a, ups[2], downs[2]))

    weights = []
    for i in (1, 2, 3):
        blocks = ups[i], downs[i]
        weights.append(merge(blocks, [send(block, dc=1) for block in blocks]))
    inner = [inner_terms(t, v_a)]
    last = after((ups[-1][:4], downs[-1][4:]), inner[0])
    opposite = jnp.concatenate([send(last[0], dz=1), send(last[1], dz=-1)], 0)

    parts = [ladder_part(inner, weights)]
    got = [send(parts[0][1], dx=2)]
    blocks = w, after(opposite, parts[0][1])
    weights.append(merge(blocks, [send(block, dc=1) for block in blocks]))
    inner.append(inner_terms(t, v_b))
    parts.append(ladder_part(inner[1:], weights[:3]))
    got.append(send(parts[1][1], dx=2))
    parts.append(ladder_part(inner, weights[3:]))
    got.append(send(parts[2][1], dx=2))
    return assemble([own for own, _ in parts], got)


def solution(mesh):
    fine = Mesh(mesh.devices.reshape(SIZES), AXES)
    return jax.shard_map(
        per_device,
        mesh=fine,
        in_specs=(P(("z", "core"), ("y", "x_lo"), None), P("pair", None, ("y", "x_lo"))),
        out_specs=P("pair", ("z", "core", "y", "x_lo"), None),
        check_vma=False,
    )
```

```python
import jax
import jax.numpy as jnp
import numpy as np
from jax import lax
from jax.experimental import pallas as pl
from jax.experimental.pallas import tpu as pltpu
from jax.sharding import Mesh, PartitionSpec as P

NC, NG = 8, 500
AXES = ("z", "core", "y", "x_lo", "pair")
SIZES = (8, 2, 4, 2, 2)
MIB = 1 << 20
F32, BF16 = jnp.float32, jnp.bfloat16
SHIFTS = ((-1, 1), (-2, 2), (-3, 3), (0, 4))


def flat(x, y, z, c):
    x, y, z, c = x % 4, y % 4, z % 8, c % 2
    return ((z * 2 + c) * 8 + (y * 2 + x % 2)) * 2 + x // 2


def send(value, dx=0, dy=0, dz=0, dc=0, only=lambda x, y: True):
    pairs = [
        (flat(x, y, z, c), flat(x + dx, y + dy, z + dz, c + dc))
        for x in range(4)
        for y in range(4)
        for z in range(8)
        for c in range(2)
        if only(x, y)
    ]
    return lax.ppermute(value, AXES, pairs)


def over_y(value):
    return lax.all_to_all(value, "y", 0, 0, tiled=True)


def after(value, *earlier):
    return lax.optimization_barrier((value, *earlier))[0]


def params(mib=24):
    return pltpu.CompilerParams(vmem_limit_bytes=mib * MIB)


def cost(flops, nbytes):
    return pl.CostEstimate(flops=flops, bytes_accessed=nbytes, transcendentals=0)


I, D = np.arange(2048) // 128, np.arange(2048) % 128
PICK = ((I[:, None] == np.arange(128) % 16) & (D[:, None] == np.arange(128) // 16)).astype(BF16)
R, K = np.arange(128), np.arange(256)


def chosen_rows(x):
    first = [8 * (o % 4 % 2) + 4 * (o % 4 // 2) for o in (x, x + 1, x + 3)]
    rows = np.array([first[0] + b for b in range(4)] + [first[1], first[1] + 1, first[2] + 2, first[2] + 3])
    return (K[None] // 16 == R[:, None] % 16) & (K[None] % 16 == rows[R // 16][:, None])


ROWS = np.stack([chosen_rows(x) for x in range(4)]).astype(BF16)


R, K = np.arange(128), np.arange(256)


def chosen_rows(x):
    first = [8 * (o % 4 % 2) + 4 * (o % 4 // 2) for o in (x, x + 1, x + 3)]
    rows = np.array([first[0] + b for b in range(4)] + [first[1], first[1] + 1, first[2] + 2, first[2] + 3])
    return (K[None] // 16 == R[:, None] % 16) & (K[None] % 16 == rows[R // 16][:, None])


ROWS = np.stack([chosen_rows(x) for x in range(4)]).astype(BF16)


def extract_kernel(lo_ref, hi_ref, pick_ref, rows_ref, *out_refs):
    w_ref, v_refs = out_refs[0], out_refs[1:]
    x = 2 * lax.axis_index("pair") + lax.axis_index("x_lo")
    first = 128 * pl.program_id(0)
    for s in range(8):
        cols = []
        halves = [lo_ref[16 * s : 16 * s + 16], hi_ref[16 * s : 16 * s + 16]]
        if s >= 6:
            g = lax.broadcasted_iota(jnp.int32, (16, 64, 128), 0) + (256 + first + 16 * s)
            halves[1] = jnp.where(g < NG, halves[1], 0)
        cols = jnp.concatenate([jnp.concatenate([h[i] for h in halves], axis=0) for i in range(16)], axis=1)
        picked = jnp.dot(cols, pick_ref[...], preferred_element_type=F32)
        w_ref[:, 16 * s : 16 * s + 16] = jnp.transpose(picked).astype(BF16).reshape(NC, 16, 128)
        for h, block in enumerate(halves):
            for y in range(4):
                chosen = block[:, 16 * y : 16 * y + 16].reshape(256, 128)
                chosen = jnp.dot(rows_ref[x], chosen, preferred_element_type=F32)
                chosen = chosen.astype(BF16).reshape(8, 16, 128)
                for (start, count), v_ref in zip(((0, 4), (4, 2), (6, 2)), v_refs):
                    v_ref[y, :, h, 16 * s : 16 * s + 16] = chosen[start : start + count]


def extract(by_g):
    return pl.pallas_call(
        extract_kernel,
        grid=(2,),
        in_specs=[
            pl.BlockSpec((128, 64, 128), lambda u: (u, 0, 0)),
            pl.BlockSpec((128, 64, 128), lambda u: (2 + u, 0, 0)),
            pl.BlockSpec((2048, 128), lambda u: (0, 0)),
            pl.BlockSpec((4, 128, 256), lambda u: (0, 0, 0)),
        ],
        out_specs=[pl.BlockSpec((NC, 128, 128), lambda u: (0, u, 0))]
        + [pl.BlockSpec((4, n, 2, 128, 128), lambda u: (0, 0, 0, u, 0)) for n in (4, 2, 2)],
        out_shape=[jax.ShapeDtypeStruct((NC, 256, 128), BF16)]
        + [jax.ShapeDtypeStruct((4, n, 2, 256, 128), BF16) for n in (8, 2, 2)],
        compiler_params=params(56),
        cost_estimate=cost(4 * 2048 * 2048 * 128, 13 * MIB),
    )(by_g, by_g, jnp.asarray(PICK), jnp.asarray(ROWS))


def amps_kernel(mine_ref, far_ref, t_ref):
    core, x_lo = lax.axis_index("core"), lax.axis_index("x_lo")
    for half, ref in ((core, mine_ref), (1 - core, far_ref)):
        for n, (side, k) in enumerate(((0, 0), (1, x_lo), (1, 1 - x_lo), (0, 1))):
            for y in range(4):
                lanes = slice((2 * y + side) * 128, (2 * y + side) * 128 + 128)
                for c in range(4):
                    t_ref[half * 4 + c, k, :, lanes] = ref[n, y, c]


def gather_amps(mine, far):
    return pl.pallas_call(
        amps_kernel,
        out_shape=jax.ShapeDtypeStruct((NC, 2, 96, 1024), BF16),
        compiler_params=params(8),
        cost_estimate=cost(0, 7 * MIB),
    )(mine, far)


def inner_kernel(first, t_ref, v_ref, out_ref, held_ref, sems):
    def copies(b):
        return [
            pltpu.make_async_copy(v_ref.at[:, 4 * n + first + b], held_ref.at[b, n], sems.at[b, n]) for n in range(2)
        ]

    for b in range(2):
        for copy in copies(b):
            copy.start()
    t = t_ref[...].reshape(NC * 192, 1024)
    for b in range(2):
        for copy in copies(b):
            copy.wait()
        v = jnp.concatenate([held_ref[b, n, y] for y in range(4) for n in range(2)], axis=-1)
        prod = lax.dot_general(t, v, (((1,), (1,)), ((), ())), preferred_element_type=F32)
        out_ref[:, b * 192 : (b + 1) * 192] = prod.astype(BF16).reshape(NC, 192, 512)


def inner_terms(t, v, first):
    def kernel(*refs):
        inner_kernel(first, *refs)

    return pl.pallas_call(
        kernel,
        in_specs=[pl.BlockSpec(memory_space=pltpu.VMEM), pl.BlockSpec(memory_space=pl.ANY)],
        out_shape=jax.ShapeDtypeStruct((NC, 2 * 192, 512), BF16),
        scratch_shapes=[pltpu.VMEM((2, 2, 4, 512, 128), BF16), pltpu.SemaphoreType.DMA((2, 2))],
        compiler_params=params(18),
        cost_estimate=cost(2 * 2 * 1536 * 1024 * 512, 8 * MIB),
    )(t, v)


def merge_kernel(mine0, mine1, far0, far1, out_ref):
    x = 2 * lax.axis_index("pair") + lax.axis_index("x_lo")
    low = lax.broadcasted_iota(jnp.int32, (256, 128), 1) < 64
    for n, (mine_ref, far_ref) in enumerate(((mine0, far0), (mine1, far1))):
        lanes = slice(n * 128, n * 128 + 128)
        for i in range(NC):
            c = i + 4 * (x // 2) - 8 * (x // 2) * (i // 4)
            mine, far = mine_ref[i].astype(F32), far_ref[i].astype(F32)
            out_ref[c, :256, lanes] = jnp.where(low, mine, pltpu.roll(far, 64, 1)).astype(BF16)
            out_ref[c, 256:, lanes] = jnp.where(low, pltpu.roll(mine, 64, 1), far).astype(BF16)


def merge(mine, far):
    return pl.pallas_call(
        merge_kernel,
        out_shape=jax.ShapeDtypeStruct((NC, 512, 256), BF16),
        compiler_params=params(6),
        cost_estimate=cost(0, 4 * MIB),
    )(*mine, *far)


def ladder_kernel(n_inner, *refs):
    inner_refs, weight_refs, (own_ref, give_ref) = refs[:n_inner], refs[n_inner:-2], refs[-2:]
    for n, w_ref in enumerate(weight_refs):
        weight = w_ref[...].reshape(NC * 512, 256)
        for m, s_ref in enumerate(inner_refs):
            lhs = jnp.concatenate([s_ref[c] for c in range(NC)], axis=1)
            total = jnp.dot(lhs, weight, preferred_element_type=F32).reshape(2, 2, 96, 256)
            own_ref[2 * m : 2 * m + 2, :, n * 256 : n * 256 + 256] = total[:, 0]
            give_ref[2 * m : 2 * m + 2, :, n * 256 : n * 256 + 256] = total[:, 1].astype(BF16)


def ladder_part(inner, weights):
    rows, cols = 2 * len(inner), 256 * len(weights)

    def kernel(*refs):
        ladder_kernel(len(inner), *refs)

    return pl.pallas_call(
        kernel,
        out_shape=(jax.ShapeDtypeStruct((rows, 96, cols), F32), jax.ShapeDtypeStruct((rows, 96, cols), BF16)),
        compiler_params=params(16),
        cost_estimate=cost(2 * rows * 192 * 4096 * cols, 8 * MIB),
    )(*inner, *weights)


P_STEP = 48
PIECES = ((0, 2, 0, 6), (2, 2, 0, 6), (0, 4, 6, 2))


def assemble_kernel(*refs):
    owns, gots, (out_ref, held_ref) = refs[:3], refs[3:6], refs[6:]
    z, pair, core = (lax.axis_index(a) for a in ("z", "pair", "core"))
    shifts = sum(SHIFTS, ())

    def place(mine, theirs, turn):
        for (row, rows, block, blocks), own_ref, got_ref in zip(PIECES, owns, gots):
            for i in range(blocks):
                for b in range(rows):
                    for first, ref in ((mine, own_ref), (theirs, got_ref)):
                        part = ref[b, :, i * 128 : i * 128 + 128].astype(F32)
                        part = pltpu.roll(part, 64, 1) if turn else part
                        at = (first + row + b) * P_STEP
                        held_ref[block + i, at : at + P_STEP] = part

    for k in range(2):
        for turn in range(2):

            @pl.when((pair == k) & (core == turn))
            def _():
                place(4 * k, 4 - 4 * k, turn)

    for i, shift in enumerate(shifts):
        lanes = pl.ds(pl.multiple_of(lax.rem(z + 8 + shift, 8) * 128, 128), 128)
        for p in range(P_STEP):
            out_ref[p, :, lanes] = held_ref[i, pl.ds(p, 8, stride=P_STEP), :]


def assemble(own, got):
    pieces = [*own, *got]
    return pl.pallas_call(
        assemble_kernel,
        grid=(96 // P_STEP,),
        in_specs=[pl.BlockSpec((p.shape[0], P_STEP, p.shape[2]), lambda i: (0, i, 0)) for p in pieces],
        out_specs=pl.BlockSpec((P_STEP, 8, 1024), lambda p: (p, 0, 0)),
        out_shape=jax.ShapeDtypeStruct((96, 8, 1024), F32),
        scratch_shapes=[pltpu.VMEM((8, 8 * P_STEP, 128), F32)],
        compiler_params=params(14),
        cost_estimate=cost(0, 6 * MIB),
    )(*pieces)


def spread_over_y(w):
    y, pair = lax.axis_index("y"), lax.axis_index("pair")
    half = lax.dynamic_slice_in_dim(w, 4 * pair, 4, 0)
    up, down, two = (send(half, dy=d, only=lambda x, y: x % 2 == 0 and y == 0) for d in (1, -1, 2))
    return jnp.where(y == 0, half, jnp.where(y == 1, up, jnp.where(y == 3, down, two)))


def spread_over_x(half):
    x_lo = lax.axis_index("x_lo")
    even = lambda x, y: x % 2 == 0
    left, right, other = (send(half, dx=d, only=even) for d in (1, -1, 2))
    return jnp.concatenate([jnp.where(x_lo == 0, half, left), jnp.where(x_lo == 0, other, right)], axis=0)


def per_device(vertex, amps):
    w_source, *rows = extract(jnp.transpose(vertex, (2, 0, 1)))
    v, right, left = (part.reshape(4, -1, 512, 128) for part in rows)
    half = spread_over_y(w_source)

    t = jnp.transpose(amps, (1, 0, 2))
    t = lax.dynamic_slice_in_dim(t, 4 * lax.axis_index("core"), 4, 0)
    t = over_y(after(jnp.broadcast_to(t, (4, 4, 96, 128)), w_source))

    right, left = send(right, dx=1), send(left, dx=-1)
    w = spread_over_x(after(half, right, left, t))
    right, left = after((right, left), w)
    v = lax.dynamic_update_slice_in_dim(v, right, 4, 1)
    v = lax.dynamic_update_slice_in_dim(v, left, 6, 1)
    v = over_y(after(v, t))

    ups, downs, weights = [w], [w], []

    def ring_step(*wait):
        up, down = after((ups[-1], downs[-1]), *wait) if wait else (ups[-1], downs[-1])
        ups.append(send(up, dz=1))
        downs.append(send(down, dz=-1))

    def add_weights(*blocks):
        weights.append(merge(blocks, [send(block, dc=1) for block in blocks]))

    ring_step()
    ring_step()
    add_weights(ups[1], downs[1])
    ring_step()
    add_weights(ups[2], downs[2])

    t = after(t, w)
    t = jnp.stack([t, *after((send(t, dx=-1), send(t, dx=1), send(t, dx=2)), ups[2], downs[2])])
    t = gather_amps(t, send(t, dc=1))

    inner = [inner_terms(t, v, 0)]
    opposite = jnp.concatenate([send(ups[3][:4], dz=1), send(downs[3][4:], dz=-1)], 0)
    add_weights(ups[3], downs[3])
    parts = [ladder_part(inner, weights)]
    got = [send(parts[0][1], dx=2)]
    inner.append(inner_terms(t, v, 2))
    add_weights(w, opposite)
    parts.append(ladder_part(inner[1:], weights[:3]))
    got.append(send(parts[1][1], dx=2))
    parts.append(ladder_part(inner, weights[3:]))
    got.append(send(parts[2][1], dx=2))
    return assemble([own for own, _ in parts], got)


def solution(mesh):
    fine = Mesh(mesh.devices.reshape(SIZES), AXES)
    return jax.shard_map(
        per_device,
        mesh=fine,
        in_specs=(P(("z", "core"), ("y", "x_lo"), None), P("pair", None, ("y", "x_lo"))),
        out_specs=P("pair", ("z", "core", "y", "x_lo"), None),
        check_vma=False,
    )
```

```python
import jax
import jax.numpy as jnp
import numpy as np
from jax import lax
from jax.experimental import pallas as pl
from jax.experimental.pallas import tpu as pltpu
from jax.sharding import Mesh, PartitionSpec as P

NC, NG = 8, 500
AXES = ("z", "core", "y", "x_lo", "pair")
SIZES = (8, 2, 4, 2, 2)
MIB = 1 << 20
F32, BF16 = jnp.float32, jnp.bfloat16
SHIFTS = ((-1, 1), (-2, 2), (-3, 3), (0, 4))


def flat(x, y, z, c):
    x, y, z, c = x % 4, y % 4, z % 8, c % 2
    return ((z * 2 + c) * 8 + (y * 2 + x % 2)) * 2 + x // 2


def send(value, dx=0, dy=0, dz=0, dc=0, only=lambda x, y: True):
    pairs = [
        (flat(x, y, z, c), flat(x + dx, y + dy, z + dz, c + dc))
        for x in range(4)
        for y in range(4)
        for z in range(8)
        for c in range(2)
        if only(x, y)
    ]
    return lax.ppermute(value, AXES, pairs)


def over_y(value):
    return lax.all_to_all(value, "y", 0, 0, tiled=True)


def after(value, *earlier):
    return lax.optimization_barrier((value, *earlier))[0]


def params(mib=24):
    return pltpu.CompilerParams(vmem_limit_bytes=mib * MIB)


def cost(flops, nbytes):
    return pl.CostEstimate(flops=flops, bytes_accessed=nbytes, transcendentals=0)


I, D = np.arange(2048) // 128, np.arange(2048) % 128
PICK = ((I[:, None] == np.arange(128) % 16) & (D[:, None] == np.arange(128) // 16)).astype(BF16)
R, K = np.arange(128), np.arange(256)


def chosen_rows(x):
    first = [8 * (o % 4 % 2) + 4 * (o % 4 // 2) for o in (x, x + 1, x + 3)]
    rows = np.array([first[0] + b for b in range(4)] + [first[1], first[1] + 1, first[2] + 2, first[2] + 3])
    return (K[None] // 16 == R[:, None] % 16) & (K[None] % 16 == rows[R // 16][:, None])


ROWS = np.stack([chosen_rows(x) for x in range(4)]).astype(BF16)


R, K = np.arange(128), np.arange(256)


def chosen_rows(x):
    first = [8 * (o % 4 % 2) + 4 * (o % 4 // 2) for o in (x, x + 1, x + 3)]
    rows = np.array([first[0] + b for b in range(4)] + [first[1], first[1] + 1, first[2] + 2, first[2] + 3])
    return (K[None] // 16 == R[:, None] % 16) & (K[None] % 16 == rows[R // 16][:, None])


ROWS = np.stack([chosen_rows(x) for x in range(4)]).astype(BF16)


def extract_kernel(lo_ref, hi_ref, pick_ref, rows_ref, *out_refs):
    w_ref, v_refs = out_refs[0], out_refs[1:]
    x = 2 * lax.axis_index("pair") + lax.axis_index("x_lo")
    first = 128 * pl.program_id(0)
    for s in range(8):
        cols = []
        halves = [lo_ref[16 * s : 16 * s + 16], hi_ref[16 * s : 16 * s + 16]]
        if s >= 6:
            g = lax.broadcasted_iota(jnp.int32, (16, 64, 128), 0) + (256 + first + 16 * s)
            halves[1] = jnp.where(g < NG, halves[1], 0)
        cols = jnp.concatenate([jnp.concatenate([h[i] for h in halves], axis=0) for i in range(16)], axis=1)
        picked = jnp.dot(cols, pick_ref[...], preferred_element_type=F32)
        w_ref[:, 16 * s : 16 * s + 16] = jnp.transpose(picked).astype(BF16).reshape(NC, 16, 128)
        for h, block in enumerate(halves):
            for y in range(4):
                chosen = block[:, 16 * y : 16 * y + 16].reshape(256, 128)
                chosen = jnp.dot(rows_ref[x], chosen, preferred_element_type=F32)
                chosen = chosen.astype(BF16).reshape(8, 16, 128)
                for (start, count), v_ref in zip(((0, 4), (4, 2), (6, 2)), v_refs):
                    v_ref[y, :, h, 16 * s : 16 * s + 16] = chosen[start : start + count]


def extract(by_g):
    return pl.pallas_call(
        extract_kernel,
        grid=(2,),
        in_specs=[
            pl.BlockSpec((128, 64, 128), lambda u: (u, 0, 0)),
            pl.BlockSpec((128, 64, 128), lambda u: (2 + u, 0, 0)),
            pl.BlockSpec((2048, 128), lambda u: (0, 0)),
            pl.BlockSpec((4, 128, 256), lambda u: (0, 0, 0)),
        ],
        out_specs=[pl.BlockSpec((NC, 128, 128), lambda u: (0, u, 0))]
        + [pl.BlockSpec((4, n, 2, 128, 128), lambda u: (0, 0, 0, u, 0)) for n in (4, 2, 2)],
        out_shape=[jax.ShapeDtypeStruct((NC, 256, 128), BF16)]
        + [jax.ShapeDtypeStruct((4, n, 2, 256, 128), BF16) for n in (8, 2, 2)],
        compiler_params=params(56),
        cost_estimate=cost(4 * 2048 * 2048 * 128, 13 * MIB),
    )(by_g, by_g, jnp.asarray(PICK), jnp.asarray(ROWS))


def amps_kernel(mine_ref, far_ref, t_ref):
    core, x_lo = lax.axis_index("core"), lax.axis_index("x_lo")
    for half, ref in ((core, mine_ref), (1 - core, far_ref)):
        for n, (side, k) in enumerate(((0, 0), (1, x_lo), (1, 1 - x_lo), (0, 1))):
            for y in range(4):
                lanes = slice((2 * y + side) * 128, (2 * y + side) * 128 + 128)
                for c in range(4):
                    t_ref[half * 4 + c, k, :, lanes] = ref[n, y, c]


def gather_amps(mine, far):
    return pl.pallas_call(
        amps_kernel,
        out_shape=jax.ShapeDtypeStruct((NC, 2, 96, 1024), BF16),
        compiler_params=params(8),
        cost_estimate=cost(0, 7 * MIB),
    )(mine, far)


def inner_kernel(t_ref, v_ref, out_ref, held_ref, sems):
    def copies(b):
        return [pltpu.make_async_copy(v_ref.at[:, 4 * n + b], held_ref.at[b, n], sems.at[b, n]) for n in range(2)]

    for b in range(4):
        for copy in copies(b):
            copy.start()
    t = t_ref[...].reshape(NC * 192, 1024)
    for b in range(4):
        for copy in copies(b):
            copy.wait()
        v = jnp.concatenate([held_ref[b, n, y] for y in range(4) for n in range(2)], axis=-1)
        prod = lax.dot_general(t, v, (((1,), (1,)), ((), ())), preferred_element_type=F32)
        out_ref[:, b * 192 : (b + 1) * 192] = prod.astype(BF16).reshape(NC, 192, 512)


def inner_terms(t, v):
    return pl.pallas_call(
        inner_kernel,
        in_specs=[pl.BlockSpec(memory_space=pltpu.VMEM), pl.BlockSpec(memory_space=pl.ANY)],
        out_shape=jax.ShapeDtypeStruct((NC, 768, 512), BF16),
        scratch_shapes=[pltpu.VMEM((4, 2, 4, 512, 128), BF16), pltpu.SemaphoreType.DMA((4, 2))],
        compiler_params=params(26),
        cost_estimate=cost(2 * 4 * 1536 * 1024 * 512, 13 * MIB),
    )(t, v)


def merge_kernel(mine0, mine1, far0, far1, out_ref):
    x = 2 * lax.axis_index("pair") + lax.axis_index("x_lo")
    low = lax.broadcasted_iota(jnp.int32, (256, 128), 1) < 64
    for n, (mine_ref, far_ref) in enumerate(((mine0, far0), (mine1, far1))):
        lanes = slice(n * 128, n * 128 + 128)
        for i in range(NC):
            c = i + 4 * (x // 2) - 8 * (x // 2) * (i // 4)
            mine, far = mine_ref[i].astype(F32), far_ref[i].astype(F32)
            out_ref[c, :256, lanes] = jnp.where(low, mine, pltpu.roll(far, 64, 1)).astype(BF16)
            out_ref[c, 256:, lanes] = jnp.where(low, pltpu.roll(mine, 64, 1), far).astype(BF16)


def merge(mine, far):
    return pl.pallas_call(
        merge_kernel,
        out_shape=jax.ShapeDtypeStruct((NC, 512, 256), BF16),
        compiler_params=params(6),
        cost_estimate=cost(0, 4 * MIB),
    )(*mine, *far)


def ladder_kernel(s_ref, w_ref, own_ref, give_ref):
    lhs = jnp.concatenate([s_ref[c] for c in range(NC)], axis=1)
    total = jnp.dot(lhs, w_ref[...].reshape(NC * 512, 256), preferred_element_type=F32)
    total = total.reshape(4, 2, 96, 256)
    own_ref[...] = total[:, 0]
    give_ref[...] = total[:, 1].astype(BF16)


def ladder_part(inner, weights):
    return pl.pallas_call(
        ladder_kernel,
        out_shape=(jax.ShapeDtypeStruct((4, 96, 256), F32), jax.ShapeDtypeStruct((4, 96, 256), BF16)),
        compiler_params=params(16),
        cost_estimate=cost(2 * 768 * 4096 * 256, 8 * MIB),
    )(inner, weights)


P_STEP = 48
PIECES = tuple((0, 4, 2 * n, 2) for n in range(4))


def assemble_kernel(*refs):
    owns, gots, (out_ref, held_ref) = refs[:4], refs[4:8], refs[8:]
    z, pair, core = (lax.axis_index(a) for a in ("z", "pair", "core"))
    shifts = sum(SHIFTS, ())

    def place(mine, theirs, turn):
        for (row, rows, block, blocks), own_ref, got_ref in zip(PIECES, owns, gots):
            for i in range(blocks):
                for b in range(rows):
                    for first, ref in ((mine, own_ref), (theirs, got_ref)):
                        part = ref[b, :, i * 128 : i * 128 + 128].astype(F32)
                        part = pltpu.roll(part, 64, 1) if turn else part
                        at = (first + row + b) * P_STEP
                        held_ref[block + i, at : at + P_STEP] = part

    for k in range(2):
        for turn in range(2):

            @pl.when((pair == k) & (core == turn))
            def _():
                place(4 * k, 4 - 4 * k, turn)

    for i, shift in enumerate(shifts):
        lanes = pl.ds(pl.multiple_of(lax.rem(z + 8 + shift, 8) * 128, 128), 128)
        for p in range(P_STEP):
            out_ref[p, :, lanes] = held_ref[i, pl.ds(p, 8, stride=P_STEP), :]


def assemble(own, got):
    pieces = [*own, *got]
    return pl.pallas_call(
        assemble_kernel,
        grid=(96 // P_STEP,),
        in_specs=[pl.BlockSpec((p.shape[0], P_STEP, p.shape[2]), lambda i: (0, i, 0)) for p in pieces],
        out_specs=pl.BlockSpec((P_STEP, 8, 1024), lambda p: (p, 0, 0)),
        out_shape=jax.ShapeDtypeStruct((96, 8, 1024), F32),
        scratch_shapes=[pltpu.VMEM((8, 8 * P_STEP, 128), F32)],
        compiler_params=params(14),
        cost_estimate=cost(0, 6 * MIB),
    )(*pieces)


def spread_over_y(w):
    y, pair = lax.axis_index("y"), lax.axis_index("pair")
    half = lax.dynamic_slice_in_dim(w, 4 * pair, 4, 0)
    up, down, two = (send(half, dy=d, only=lambda x, y: x % 2 == 0 and y == 0) for d in (1, -1, 2))
    return jnp.where(y == 0, half, jnp.where(y == 1, up, jnp.where(y == 3, down, two)))


def spread_over_x(half):
    x_lo = lax.axis_index("x_lo")
    even = lambda x, y: x % 2 == 0
    left, right, other = (send(half, dx=d, only=even) for d in (1, -1, 2))
    return jnp.concatenate([jnp.where(x_lo == 0, half, left), jnp.where(x_lo == 0, other, right)], axis=0)


def per_device(vertex, amps):
    w_source, *rows = extract(jnp.transpose(vertex, (2, 0, 1)))
    v, right, left = (part.reshape(4, -1, 512, 128) for part in rows)
    half = spread_over_y(w_source)

    t = jnp.transpose(amps, (1, 0, 2))
    t = lax.dynamic_slice_in_dim(t, 4 * lax.axis_index("core"), 4, 0)
    t = over_y(after(jnp.broadcast_to(t, (4, 4, 96, 128)), w_source))

    right, left = send(right, dx=1), send(left, dx=-1)
    w = spread_over_x(after(half, right, left, t))
    right, left = after((right, left), w)
    v = lax.dynamic_update_slice_in_dim(v, right, 4, 1)
    v = lax.dynamic_update_slice_in_dim(v, left, 6, 1)
    v = over_y(after(v, t))

    ups, downs, weights = [w], [w], []

    def ring_step(*wait):
        up, down = after((ups[-1], downs[-1]), *wait) if wait else (ups[-1], downs[-1])
        ups.append(send(up, dz=1))
        downs.append(send(down, dz=-1))

    def add_weights(*blocks):
        weights.append(merge(blocks, [send(block, dc=1) for block in blocks]))

    ring_step()
    ring_step()
    add_weights(ups[1], downs[1])
    ring_step()
    add_weights(ups[2], downs[2])

    t = after(t, w)
    t = jnp.stack([t, *after((send(t, dx=-1), send(t, dx=1), send(t, dx=2)), ups[2], downs[2])])
    t = gather_amps(t, send(t, dc=1))

    inner = inner_terms(t, v)
    opposite = jnp.concatenate([send(ups[3][:4], dz=1), send(downs[3][4:], dz=-1)], 0)
    add_weights(ups[3], downs[3])
    add_weights(w, opposite)
    parts = [ladder_part(inner, weight) for weight in weights]
    return assemble([own for own, _ in parts], [send(give, dx=2) for _, give in parts])


def solution(mesh):
    fine = Mesh(mesh.devices.reshape(SIZES), AXES)
    return jax.shard_map(
        per_device,
        mesh=fine,
        in_specs=(P(("z", "core"), ("y", "x_lo"), None), P("pair", None, ("y", "x_lo"))),
        out_specs=P("pair", ("z", "core", "y", "x_lo"), None),
        check_vma=False,
    )
```

```python
import jax
import jax.numpy as jnp
import numpy as np
from jax import lax
from jax.experimental import pallas as pl
from jax.experimental.pallas import tpu as pltpu
from jax.sharding import Mesh, PartitionSpec as P

NC, NG = 8, 500
AXES = ("z", "core", "y", "x_lo", "pair")
SIZES = (8, 2, 4, 2, 2)
MIB = 1 << 20
F32, BF16 = jnp.float32, jnp.bfloat16
SHIFTS = ((-1, 1), (-2, 2), (-3, 3), (0, 4))


def flat(x, y, z, c):
    x, y, z, c = x % 4, y % 4, z % 8, c % 2
    return ((z * 2 + c) * 8 + (y * 2 + x % 2)) * 2 + x // 2


def send(value, dx=0, dy=0, dz=0, dc=0, only=lambda x, y: True):
    pairs = [
        (flat(x, y, z, c), flat(x + dx, y + dy, z + dz, c + dc))
        for x in range(4)
        for y in range(4)
        for z in range(8)
        for c in range(2)
        if only(x, y)
    ]
    return lax.ppermute(value, AXES, pairs)


def over_y(value):
    return lax.all_to_all(value, "y", 0, 0, tiled=True)


def after(value, *earlier):
    return lax.optimization_barrier((value, *earlier))[0]


def params(mib=24):
    return pltpu.CompilerParams(vmem_limit_bytes=mib * MIB)


def cost(flops, nbytes):
    return pl.CostEstimate(flops=flops, bytes_accessed=nbytes, transcendentals=0)


I, D = np.arange(2048) // 128, np.arange(2048) % 128
PICK = ((I[:, None] == np.arange(128) % 16) & (D[:, None] == np.arange(128) // 16)).astype(BF16)
R, K = np.arange(128), np.arange(256)


def chosen_rows(x):
    first = [8 * (o % 4 % 2) + 4 * (o % 4 // 2) for o in (x, x + 1, x + 3)]
    rows = np.array([first[0] + b for b in range(4)] + [first[1], first[1] + 1, first[2] + 2, first[2] + 3])
    return (K[None] // 16 == R[:, None] % 16) & (K[None] % 16 == rows[R // 16][:, None])


ROWS = np.stack([chosen_rows(x) for x in range(4)]).astype(BF16)


R, K = np.arange(128), np.arange(256)


def chosen_rows(x):
    first = [8 * (o % 4 % 2) + 4 * (o % 4 // 2) for o in (x, x + 1, x + 3)]
    rows = np.array([first[0] + b for b in range(4)] + [first[1], first[1] + 1, first[2] + 2, first[2] + 3])
    return (K[None] // 16 == R[:, None] % 16) & (K[None] % 16 == rows[R // 16][:, None])


ROWS = np.stack([chosen_rows(x) for x in range(4)]).astype(BF16)


def extract_kernel(lo_ref, hi_ref, pick_ref, rows_ref, *out_refs):
    w_ref, v_refs = out_refs[0], out_refs[1:]
    x = 2 * lax.axis_index("pair") + lax.axis_index("x_lo")
    first = 128 * pl.program_id(0)
    for s in range(8):
        cols = []
        halves = [lo_ref[16 * s : 16 * s + 16], hi_ref[16 * s : 16 * s + 16]]
        if s >= 6:
            g = lax.broadcasted_iota(jnp.int32, (16, 64, 128), 0) + (256 + first + 16 * s)
            halves[1] = jnp.where(g < NG, halves[1], 0)
        cols = jnp.concatenate([jnp.concatenate([h[i] for h in halves], axis=0) for i in range(16)], axis=1)
        picked = jnp.dot(cols, pick_ref[...], preferred_element_type=F32)
        w_ref[:, 16 * s : 16 * s + 16] = jnp.transpose(picked).astype(BF16).reshape(NC, 16, 128)
        for h, block in enumerate(halves):
            for y in range(4):
                chosen = block[:, 16 * y : 16 * y + 16].reshape(256, 128)
                chosen = jnp.dot(rows_ref[x], chosen, preferred_element_type=F32)
                chosen = chosen.astype(BF16).reshape(8, 16, 128)
                for (start, count), v_ref in zip(((0, 4), (4, 2), (6, 2)), v_refs):
                    v_ref[y, :, h, 16 * s : 16 * s + 16] = chosen[start : start + count]


def extract(by_g):
    return pl.pallas_call(
        extract_kernel,
        grid=(2,),
        in_specs=[
            pl.BlockSpec((128, 64, 128), lambda u: (u, 0, 0)),
            pl.BlockSpec((128, 64, 128), lambda u: (2 + u, 0, 0)),
            pl.BlockSpec((2048, 128), lambda u: (0, 0)),
            pl.BlockSpec((4, 128, 256), lambda u: (0, 0, 0)),
        ],
        out_specs=[pl.BlockSpec((NC, 128, 128), lambda u: (0, u, 0))]
        + [pl.BlockSpec((4, n, 2, 128, 128), lambda u: (0, 0, 0, u, 0)) for n in (4, 2, 2)],
        out_shape=[jax.ShapeDtypeStruct((NC, 256, 128), BF16)]
        + [jax.ShapeDtypeStruct((4, n, 2, 256, 128), BF16) for n in (8, 2, 2)],
        compiler_params=params(56),
        cost_estimate=cost(4 * 2048 * 2048 * 128, 13 * MIB),
    )(by_g, by_g, jnp.asarray(PICK), jnp.asarray(ROWS))


def amps_kernel(mine_ref, far_ref, t_ref):
    core, x_lo = lax.axis_index("core"), lax.axis_index("x_lo")
    for half, ref in ((core, mine_ref), (1 - core, far_ref)):
        for n, (side, k) in enumerate(((0, 0), (1, x_lo), (1, 1 - x_lo), (0, 1))):
            for y in range(4):
                lanes = slice((2 * y + side) * 128, (2 * y + side) * 128 + 128)
                for c in range(4):
                    t_ref[half * 4 + c, k, :, lanes] = ref[n, y, c]


def gather_amps(mine, far):
    return pl.pallas_call(
        amps_kernel,
        out_shape=jax.ShapeDtypeStruct((NC, 2, 96, 1024), BF16),
        compiler_params=params(8),
        cost_estimate=cost(0, 7 * MIB),
    )(mine, far)


def inner_kernel(first, t_ref, v_ref, out_ref, held_ref, sems):
    def copies(b):
        return [
            pltpu.make_async_copy(v_ref.at[:, 4 * n + first + b], held_ref.at[b, n], sems.at[b, n]) for n in range(2)
        ]

    for b in range(2):
        for copy in copies(b):
            copy.start()
    t = t_ref[...].reshape(NC * 192, 1024)
    for b in range(2):
        for copy in copies(b):
            copy.wait()
        v = jnp.concatenate([held_ref[b, n, y] for y in range(4) for n in range(2)], axis=-1)
        prod = lax.dot_general(t, v, (((1,), (1,)), ((), ())), preferred_element_type=F32)
        out_ref[:, b * 192 : (b + 1) * 192] = prod.astype(BF16).reshape(NC, 192, 512)


def inner_terms(t, v, first):
    def kernel(*refs):
        inner_kernel(first, *refs)

    return pl.pallas_call(
        kernel,
        in_specs=[pl.BlockSpec(memory_space=pltpu.VMEM), pl.BlockSpec(memory_space=pl.ANY)],
        out_shape=jax.ShapeDtypeStruct((NC, 2 * 192, 512), BF16),
        scratch_shapes=[pltpu.VMEM((2, 2, 4, 512, 128), BF16), pltpu.SemaphoreType.DMA((2, 2))],
        compiler_params=params(18),
        cost_estimate=cost(2 * 2 * 1536 * 1024 * 512, 8 * MIB),
    )(t, v)


def merge_kernel(mine0, mine1, far0, far1, out_ref):
    x = 2 * lax.axis_index("pair") + lax.axis_index("x_lo")
    low = lax.broadcasted_iota(jnp.int32, (256, 128), 1) < 64
    for n, (mine_ref, far_ref) in enumerate(((mine0, far0), (mine1, far1))):
        lanes = slice(n * 128, n * 128 + 128)
        for i in range(NC):
            c = i + 4 * (x // 2) - 8 * (x // 2) * (i // 4)
            mine, far = mine_ref[i].astype(F32), far_ref[i].astype(F32)
            out_ref[c, :256, lanes] = jnp.where(low, mine, pltpu.roll(far, 64, 1)).astype(BF16)
            out_ref[c, 256:, lanes] = jnp.where(low, pltpu.roll(mine, 64, 1), far).astype(BF16)


def merge(mine, far):
    return pl.pallas_call(
        merge_kernel,
        out_shape=jax.ShapeDtypeStruct((NC, 512, 256), BF16),
        compiler_params=params(6),
        cost_estimate=cost(0, 4 * MIB),
    )(*mine, *far)


def ladder_kernel(n_inner, *refs):
    inner_refs, weight_refs, (own_ref, give_ref) = refs[:n_inner], refs[n_inner:-2], refs[-2:]
    for n, w_ref in enumerate(weight_refs):
        weight = w_ref[...].reshape(NC * 512, 256)
        for m, s_ref in enumerate(inner_refs):
            lhs = jnp.concatenate([s_ref[c] for c in range(NC)], axis=1)
            total = jnp.dot(lhs, weight, preferred_element_type=F32).reshape(2, 2, 96, 256)
            own_ref[2 * m : 2 * m + 2, :, n * 256 : n * 256 + 256] = total[:, 0]
            give_ref[2 * m : 2 * m + 2, :, n * 256 : n * 256 + 256] = total[:, 1].astype(BF16)


def ladder_part(inner, weights):
    rows, cols = 2 * len(inner), 256 * len(weights)

    def kernel(*refs):
        ladder_kernel(len(inner), *refs)

    return pl.pallas_call(
        kernel,
        out_shape=(jax.ShapeDtypeStruct((rows, 96, cols), F32), jax.ShapeDtypeStruct((rows, 96, cols), BF16)),
        compiler_params=params(16),
        cost_estimate=cost(2 * rows * 192 * 4096 * cols, 8 * MIB),
    )(*inner, *weights)


P_STEP = 48
PIECES = ((0, 2, 0, 6), (2, 2, 0, 6), (0, 4, 6, 2))


def assemble_kernel(*refs):
    owns, gots, (out_ref, held_ref) = refs[:3], refs[3:6], refs[6:]
    z, pair, core = (lax.axis_index(a) for a in ("z", "pair", "core"))
    shifts = sum(SHIFTS, ())

    def place(mine, theirs, turn):
        for (row, rows, block, blocks), own_ref, got_ref in zip(PIECES, owns, gots):
            for i in range(blocks):
                for b in range(rows):
                    for first, ref in ((mine, own_ref), (theirs, got_ref)):
                        part = ref[b, :, i * 128 : i * 128 + 128].astype(F32)
                        part = pltpu.roll(part, 64, 1) if turn else part
                        at = (first + row + b) * P_STEP
                        held_ref[block + i, at : at + P_STEP] = part

    for k in range(2):
        for turn in range(2):

            @pl.when((pair == k) & (core == turn))
            def _():
                place(4 * k, 4 - 4 * k, turn)

    for i, shift in enumerate(shifts):
        lanes = pl.ds(pl.multiple_of(lax.rem(z + 8 + shift, 8) * 128, 128), 128)
        for p in range(P_STEP):
            out_ref[p, :, lanes] = held_ref[i, pl.ds(p, 8, stride=P_STEP), :]


def assemble(own, got):
    pieces = [*own, *got]
    return pl.pallas_call(
        assemble_kernel,
        grid=(96 // P_STEP,),
        in_specs=[pl.BlockSpec((p.shape[0], P_STEP, p.shape[2]), lambda i: (0, i, 0)) for p in pieces],
        out_specs=pl.BlockSpec((P_STEP, 8, 1024), lambda p: (p, 0, 0)),
        out_shape=jax.ShapeDtypeStruct((96, 8, 1024), F32),
        scratch_shapes=[pltpu.VMEM((8, 8 * P_STEP, 128), F32)],
        compiler_params=params(14),
        cost_estimate=cost(0, 6 * MIB),
    )(*pieces)


def spread_over_y(w):
    y, pair = lax.axis_index("y"), lax.axis_index("pair")
    half = lax.dynamic_slice_in_dim(w, 4 * pair, 4, 0)
    up, down, two = (send(half, dy=d, only=lambda x, y: x % 2 == 0 and y == 0) for d in (1, -1, 2))
    return jnp.where(y == 0, half, jnp.where(y == 1, up, jnp.where(y == 3, down, two)))


def spread_over_x(half):
    x_lo = lax.axis_index("x_lo")
    even = lambda x, y: x % 2 == 0
    left, right, other = (send(half, dx=d, only=even) for d in (1, -1, 2))
    return jnp.concatenate([jnp.where(x_lo == 0, half, left), jnp.where(x_lo == 0, other, right)], axis=0)


def per_device(vertex, amps):
    w_source, *rows = extract(jnp.transpose(vertex, (2, 0, 1)))
    v, right, left = (part.reshape(4, -1, 512, 128) for part in rows)
    half = spread_over_y(w_source)

    t = jnp.transpose(amps, (1, 0, 2))
    t = lax.dynamic_slice_in_dim(t, 4 * lax.axis_index("core"), 4, 0)
    t = over_y(after(jnp.broadcast_to(t, (4, 4, 96, 128)), w_source))

    right, left = send(right, dx=1), send(left, dx=-1)
    w = spread_over_x(after(half, right, left, t))
    v = lax.dynamic_update_slice_in_dim(v, right, 4, 1)
    v = lax.dynamic_update_slice_in_dim(v, left, 6, 1)
    v = over_y(after(v, t, w))

    ups, downs, weights = [w], [w], []

    def ring_step(*wait):
        up, down = after((ups[-1], downs[-1]), *wait) if wait else (ups[-1], downs[-1])
        ups.append(send(up, dz=1))
        downs.append(send(down, dz=-1))

    def add_weights(*blocks):
        weights.append(merge(blocks, [send(block, dc=1) for block in blocks]))

    ring_step()
    ring_step()
    add_weights(ups[1], downs[1])
    ring_step()
    add_weights(ups[2], downs[2])

    t = after(t, w)
    t = jnp.stack([t, *after((send(t, dx=-1), send(t, dx=1), send(t, dx=2)), ups[2], downs[2])])
    t = gather_amps(t, send(t, dc=1))

    inner = [inner_terms(t, v, 0)]
    opposite = jnp.concatenate([send(ups[3][:4], dz=1), send(downs[3][4:], dz=-1)], 0)
    add_weights(ups[3], downs[3])
    parts = [ladder_part(inner, weights)]
    got = [send(parts[0][1], dx=2)]
    inner.append(inner_terms(t, v, 2))
    add_weights(w, opposite)
    parts.append(ladder_part(inner[1:], weights[:3]))
    got.append(send(parts[1][1], dx=2))
    parts.append(ladder_part(inner, weights[3:]))
    got.append(send(parts[2][1], dx=2))
    return assemble([own for own, _ in parts], got)


def solution(mesh):
    fine = Mesh(mesh.devices.reshape(SIZES), AXES)
    return jax.shard_map(
        per_device,
        mesh=fine,
        in_specs=(P(("z", "core"), ("y", "x_lo"), None), P("pair", None, ("y", "x_lo"))),
        out_specs=P("pair", ("z", "core", "y", "x_lo"), None),
        check_vma=False,
    )
```
